256 devices in a mesh: tm: 64 (over z, x, core), rows: 4 (over y).
Axes of the slice: x: 4, y: 4, z: 8, core: 2. Of those that a mesh axis runs over, the one named last changes fastest.
Arguments:
- sensed_flows_levels: float32 [256, 512], P('tm'), may hold values from -6 to 6
- reading_mask: int32 [256, 512], P('tm'), may hold values 0 or 1
- inventory_propagator: float32 [1024, 1024], replicated, may hold values from -1 to 1
- observation_matrix: float32 [512, 1024], replicated, may hold values from -0.1875 to 0.1875
- measurement_weight: float32 [512], replicated, may hold values from 0.05 to 0.3
- diagonal_blend_factor: float32 [256, 1024], P('tm', 'rows'), may hold values from 0 to 1
- prior_inventory_mean: float32 [1024], replicated, may hold values from -6 to 6
Outputs:
- updated_inventory_means: float32 [256, 1024], P('tm', 'rows')
- reconciled_inventories: float32 [256, 1024], P('tm', 'rows')
The draws below stay inside these ranges and needn't reach their ends.
All inputs are finite; a program needn't handle non-finite values. No bound on the sum of `reading_mask` on one device may be relied on, other than what follows from the above.
Results may differ from the reference program's by a relative error of at most 0.0003.
Values sent between devices are 32-bit elements; how exact they have to be, the bound alone decides.
No kernel may reach another device: no remote copies, remote signals or barrier semaphores. Data moves between devices by JAX's collectives and lax.ppermute only.
A program may use at most 64 MiB of HBM per device.

```python
import jax
import jax.numpy as jnp
from jax import lax

N = 1024
MEASURE_COUNT = 512
STEPS_DEV = 4
TOTAL_STEPS = 256


def draw_inventory_propagator(key, part):
    first_key, second_key = jax.random.split(key)
    diagonal = jax.random.uniform(first_key, (N, 1), jnp.float32, 0.994, 0.998)
    limit = 0.002 / N
    mixing = jnp.clip(jax.random.normal(second_key, (N, N), jnp.float32) * (0.5 * limit), -limit, limit)
    row_ids = jax.lax.broadcasted_iota(jnp.int32, (N, N), 0)
    col_ids = jax.lax.broadcasted_iota(jnp.int32, (N, N), 1)
    return jnp.where(row_ids == col_ids, diagonal, mixing)


def draw_diagonal_blend_factor(key, part):
    random_keys = jax.random.split(key, 6)
    slow_share = 4
    slow_flag = jax.random.randint(random_keys[0], (1, N), 0, 8) < slow_share
    slow_rate = 1.4 * jax.random.uniform(random_keys[1], (1, N), jnp.float32, 0.5, 1.0) / TOTAL_STEPS
    fast_rate = 2.302585 / jax.random.uniform(random_keys[2], (1, N), jnp.float32, 30.0, 50.0)
    rate = jnp.where(slow_flag, slow_rate, fast_rate)
    block_factor = jax.random.uniform(random_keys[3], (TOTAL_STEPS // STEPS_DEV, 1, 1), jnp.float32, 0.5, 2.0)
    block_factor = jnp.broadcast_to(block_factor, (TOTAL_STEPS // STEPS_DEV, STEPS_DEV, N)).reshape(TOTAL_STEPS, N)
    gain_vector = jnp.exp(-rate * block_factor)
    surge_flag = jax.random.randint(random_keys[4], (TOTAL_STEPS, 1), 0, TOTAL_STEPS) < 3
    surge_length = jax.random.uniform(random_keys[5], (TOTAL_STEPS, 1), jnp.float32, 0.5, 0.8)
    return gain_vector * jnp.where(surge_flag, surge_length, 1.0)


def touch_ends(result, key, low, largest):
    spot = [jax.random.randint(jax.random.fold_in(key, axis), (), 0, length) for axis, length in enumerate(result.shape)]
    widest = result.shape.index(max(result.shape))
    neighbour = spot[:widest] + [(spot[widest] + 1) % result.shape[widest]] + spot[widest + 1:]
    return result.at[tuple(spot)].set(low).at[tuple(neighbour)].set(largest)


def block_levels(key, dims, pieces, low, largest):
    factor_of = 1.0
    for axis_at, parts in pieces:
        steps = jax.random.uniform(jax.random.fold_in(jax.random.fold_in(key, 6), axis_at), (parts,), jnp.float32, low / len(pieces), largest / len(pieces))
        factor_of = factor_of * jnp.repeat(jnp.exp(steps), dims[axis_at] // parts).reshape((-1,) + (1,) * (len(dims) - 1 - axis_at))
    return factor_of


def bell_draw(own_key, extent, deviation, most, shards=(), kind=jnp.bfloat16):
    entries = deviation * jax.random.normal(own_key, extent, jnp.float32)
    if shards:
        entries = entries * block_levels(own_key, extent, shards, -0.22, 0.18)
    return jnp.clip(entries, -most, most).astype(kind)


def setup_inputs(seed: int = 0) -> dict:
    streams_of = jax.random.split(jax.random.key(seed), 8)
    return {
        "sensed_flows_levels": bell_draw(streams_of[0], (TOTAL_STEPS, MEASURE_COUNT), 1.0, 6.0, ((0, 64),), jnp.float32),
        "reading_mask": touch_ends((jax.random.randint(streams_of[1], (TOTAL_STEPS, MEASURE_COUNT), 0, 4) < 3).astype(jnp.int32), jax.random.fold_in(streams_of[1], 1), 0, 1),
        "inventory_propagator": draw_inventory_propagator(jax.random.fold_in(streams_of[7], 71), 0),
        "observation_matrix": bell_draw(streams_of[3], (MEASURE_COUNT, N), N ** -0.5, 0.1875, (), jnp.float32),
        "measurement_weight": jnp.clip(jax.random.uniform(streams_of[4], (MEASURE_COUNT,), jnp.float32, 0.05, 0.3), 0.05, 0.3),
        "diagonal_blend_factor": draw_diagonal_blend_factor(jax.random.fold_in(streams_of[7], 71), 0),
        "prior_inventory_mean": bell_draw(streams_of[6], (N,), 1.0, 6.0, (), jnp.float32),
    }


precise = lax.Precision.HIGHEST


def linear_map_apply(matrix, vector):
    return jnp.dot(matrix, vector, precision=precise, preferred_element_type=jnp.float32)


def reference(sensed_flows_levels, reading_mask, inventory_propagator, observation_matrix, measurement_weight, diagonal_blend_factor, prior_inventory_mean):
    blending_coefficients = reading_mask.astype(jnp.float32) * measurement_weight[None, :]

    def onward_pass_recursion(propagated_mean, inputs):
        measured, weight_row = inputs
        innovation = weight_row * (measured - linear_map_apply(observation_matrix, propagated_mean))
        current_mean = propagated_mean + jnp.dot(innovation, observation_matrix, precision=precise, preferred_element_type=jnp.float32)
        following = linear_map_apply(inventory_propagator, current_mean)
        return following, (current_mean, following)

    ignored_placeholder, (updated_inventory_means, prior_mean_single) = lax.scan(onward_pass_recursion, linear_map_apply(inventory_propagator, prior_inventory_mean), (sensed_flows_levels, blending_coefficients))

    def reverse_pass_recursion(later, inputs):
        state, propagated_mean, gain_vector = inputs
        current_mean = state + gain_vector * (later - propagated_mean)
        return current_mean, current_mean

    ignored_placeholder, reconciled_inventories = lax.scan(reverse_pass_recursion, prior_mean_single[-1], (updated_inventory_means, prior_mean_single, diagonal_blend_factor), reverse=True)
    return updated_inventory_means, reconciled_inventories
```

```python
import functools

import jax
import jax.numpy as jnp
from jax import lax
from jax.experimental import pallas as pl
from jax.experimental.pallas import tpu as pltpu
from jax.sharding import Mesh, PartitionSpec as P

F32 = jnp.float32
TIME = ("z", "x", "c")
ALL = TIME + ("y",)
VMEM = pl.BlockSpec(memory_space=pltpu.VMEM)
SMEM = pl.BlockSpec(memory_space=pltpu.SMEM)


def wide(row):
    return jnp.broadcast_to(row, (8, 128))


def tree(terms):
    while len(terms) > 1:
        terms = [a + b for a, b in zip(terms[::2], terms[1::2])]
    return terms[0]


def column_sums(blocks):
    return jnp.concatenate([jnp.sum(b, axis=0, keepdims=True) for b in blocks], 0)


def propagate(f_ref, x, diff):
    xs = [wide(x[t : t + 1]) for t in range(8)]
    out = []
    for t in range(8):
        spread = None
        for b in range(16):
            i = 8 * (16 * t + b)
            s = tree([f_ref[i : i + 8, 128 * u : 128 * u + 128] * xs[u] for u in range(8)])
            s = wide(jnp.sum(s, axis=1, keepdims=True))
            spread = jnp.where(diff == 8 * b, s, 0.0 if spread is None else spread)
        out.append(spread)
    return column_sums(out)


def update(h_ref, hw_ref, bits_ref, group, bit, z, p, diff):
    ps = [wide(p[t : t + 1]) for t in range(8)]
    zs = [wide(z[q : q + 1]) for q in range(4)]
    acc = [jnp.zeros((8, 128), F32) for _ in range(8)]
    for i in range(64):
        r = slice(8 * i, 8 * i + 8)
        s = tree([h_ref[r, 128 * t : 128 * t + 128] * ps[t] for t in range(8)])
        s = jnp.where(diff == 8 * (i % 16), zs[i // 16], 0.0) - s
        s = wide(jnp.sum(s, axis=1, keepdims=True))
        v = jnp.where((bits_ref[group, r, :] & bit) != 0, s, 0.0)
        acc = [acc[t] + hw_ref[r, 128 * t : 128 * t + 128] * v for t in range(8)]
    return p + column_sums(acc)


def filter_kernel(steps, at_ref, z_ref, bits_ref, f_ref, h_ref, hw_ref, s_ref, x_out, f_out, xh, ph):
    diff = lax.broadcasted_iota(jnp.int32, (8, 128), 1) - lax.broadcasted_iota(jnp.int32, (8, 128), 0)

    def step(k, x):
        p = propagate(f_ref, x, diff)
        ph[k] = p
        x = update(h_ref, hw_ref, bits_ref, k // 32, jnp.int32(1) << (k % 32), z_ref[k], p, diff)
        xh[k] = x
        return x

    x = lax.fori_loop(0, steps, step, s_ref[...])
    ph[steps] = propagate(f_ref, x, diff)
    at = at_ref[0]
    for j in range(4):
        x_out[j] = xh[at + j]
        f_out[j] = ph[at + j + 1]


def run_filter(at, z, bits, f, h, hw, s):
    steps = z.shape[0]
    return pl.pallas_call(
        functools.partial(filter_kernel, steps),
        out_shape=(jax.ShapeDtypeStruct((4, 8, 128), F32),) * 2,
        in_specs=[SMEM] + [VMEM] * 6,
        out_specs=(VMEM, VMEM),
        scratch_shapes=[pltpu.VMEM((steps, 8, 128), F32), pltpu.VMEM((steps + 1, 8, 128), F32)],
        compiler_params=pltpu.CompilerParams(vmem_limit_bytes=40 * 2**20),
        name="filter_all",
    )(at, z, bits, f, h, hw, s)


def smooth_kernel(at_ref, parts_ref, d_ref, x_ref, f_ref, out_ref):
    at = at_ref[0]
    later = f_ref[3]
    count = parts_ref.shape[0]

    def one(i, later):
        j = count - 1 - i
        e = parts_ref[j]
        return jnp.where(j > at, e[0:2] * later + e[2:4], later)

    later = lax.fori_loop(0, count, one, later)
    for j in reversed(range(4)):
        later = x_ref[j] + d_ref[j] * (later - f_ref[j])
        out_ref[j] = later


def body(z, mask, f, h, weight, d, prior):
    at = lax.axis_index(TIME)
    y = lax.axis_index("y")
    own = jnp.concatenate([z, mask.astype(F32)], 0)
    own = lax.dynamic_slice_in_dim(own, 128 * y, 128, 1)
    sent = jnp.broadcast_to(own[None], (256, 8, 128))
    got = lax.all_to_all(sent, ALL, 0, 0, tiled=True)
    got = got.reshape(64, 4, 2, 4, 128)
    z_all = jnp.transpose(got[:, :, 0], (0, 2, 1, 3)).reshape(256, 4, 128)
    m_all = jnp.transpose(got[:, :, 1], (0, 2, 1, 3)).reshape(8, 32, 512).astype(jnp.int32)
    bits = jnp.sum(m_all << lax.broadcasted_iota(jnp.int32, (8, 32, 512), 1), axis=1)
    bits = jnp.broadcast_to(bits[:, :, None], (8, 512, 128))
    x4, f4 = run_filter(
        (4 * at).reshape(1), z_all, bits, f, h, h * weight[:, None], prior.reshape(8, 128)
    )
    x4 = lax.dynamic_slice_in_dim(x4, 2 * y, 2, 1)
    f4 = lax.dynamic_slice_in_dim(f4, 2 * y, 2, 1)
    d4 = d.reshape(4, 2, 128)
    last = at == 63
    factor = jnp.ones((2, 128), F32)
    const = jnp.where(last, f4[3], 0.0)
    for j in reversed(range(4)):
        const = x4[j] + d4[j] * (const - f4[j])
        factor = factor * d4[j]
    element = jnp.concatenate([jnp.where(last, 0.0, factor), const], 0)
    parts = lax.all_to_all(jnp.broadcast_to(element[None], (64, 4, 128)), TIME, 0, 0, tiled=True)
    smooth = pl.pallas_call(
        smooth_kernel,
        out_shape=jax.ShapeDtypeStruct((4, 2, 128), F32),
        in_specs=[SMEM] + [VMEM] * 4,
        out_specs=VMEM,
        name="smooth_own",
    )(at.reshape(1), parts, d4, x4, f4)
    return x4.reshape(4, 256), smooth.reshape(4, 256)


def solution(mesh):
    fine = Mesh(mesh.devices.reshape(8, 4, 2, 4), ALL)
    t = P(TIME, None)
    ty = P(TIME, "y")
    return jax.shard_map(
        body,
        mesh=fine,
        in_specs=(t, t, P(), P(), P(), ty, P()),
        out_specs=(ty, ty),
        check_vma=False,
    )
```

```python
import functools

import jax
import jax.numpy as jnp
from jax import lax
from jax.experimental import pallas as pl
from jax.experimental.pallas import tpu as pltpu
from jax.sharding import Mesh, PartitionSpec as P

F32 = jnp.float32
HALF = ("l", "x", "c", "y")
PLANE = ("x", "c", "y")
TIME = ("h", "l", "x", "c")
BF16 = jnp.bfloat16
VMEM = pl.BlockSpec(memory_space=pltpu.VMEM)
SMEM = pl.BlockSpec(memory_space=pltpu.SMEM)


def wide(row):
    return jnp.broadcast_to(row, (8, 128))


def tree(terms):
    while len(terms) > 1:
        terms = [a + b for a, b in zip(terms[::2], terms[1::2])]
    return terms[0]


def column_sums(blocks):
    return jnp.concatenate([jnp.sum(b, axis=0, keepdims=True) for b in blocks], 0)


def propagate(f_ref, x, diff):
    xs = [wide(x[t : t + 1]) for t in range(8)]
    out = []
    for t in range(8):
        spread = None
        for b in range(16):
            i = 8 * (16 * t + b)
            s = tree([f_ref[i : i + 8, 128 * u : 128 * u + 128] * xs[u] for u in range(8)])
            s = wide(jnp.sum(s, axis=1, keepdims=True))
            spread = jnp.where(diff == 8 * b, s, 0.0 if spread is None else spread)
        out.append(spread)
    return column_sums(out)


def update(h_ref, hw_ref, bits_ref, bit, z, p, diff):
    ps = [wide(p[t : t + 1]) for t in range(8)]
    zs = [wide(z[q : q + 1]) for q in range(4)]
    acc = [jnp.zeros((8, 128), F32) for _ in range(8)]
    for i in range(64):
        r = slice(8 * i, 8 * i + 8)
        s = tree([h_ref[r, 128 * t : 128 * t + 128] * ps[t] for t in range(8)])
        s = jnp.where(diff == 8 * (i % 16), zs[i // 16], 0.0) - s
        s = wide(jnp.sum(s, axis=1, keepdims=True))
        v = jnp.where((bits_ref[r, :] & bit) != 0, s, 0.0)
        acc = [acc[t] + hw_ref[r, 128 * t : 128 * t + 128] * v for t in range(8)]
    return p + column_sums(acc)


def spread_index():
    return lax.broadcasted_iota(jnp.int32, (8, 128), 1) - lax.broadcasted_iota(jnp.int32, (8, 128), 0)


def halves(x):
    hi = x.astype(BF16)
    return hi, (x - hi.astype(F32)).astype(BF16)


def product(x, hi_ref, lo_ref):
    n = x.shape[0]
    hi, lo = halves(x)
    both = jnp.dot(jnp.concatenate([hi, lo], 0), hi_ref[...], preferred_element_type=F32)
    return both[:n] + both[n:] + jnp.dot(hi, lo_ref[...], preferred_element_type=F32)


def on_rows(words, i, diff):
    q = i // 16
    return wide(jnp.sum(jnp.where(diff == 8 * (i % 16), wide(words[q : q + 1]), 0.0), axis=1, keepdims=True))


def store_bits(bits_ref, words, diff):
    for i in range(64):
        bits_ref[8 * i : 8 * i + 8, :] = on_rows(words, i, diff).astype(jnp.int32)


def store_weighted(hw_ref, h_ref, weight, diff):
    for i in range(64):
        r = slice(8 * i, 8 * i + 8)
        w = on_rows(weight, i, diff)
        for t in range(8):
            c = slice(128 * t, 128 * t + 128)
            hw_ref[r, c] = h_ref[r, c] * w


def prepare_kernel(f_ref, h_ref, gp_hi, gp_lo, gy_hi, gy_lo, h_hi, h_lo, diag_ref, t_hi, t_lo):
    h_hi[...], h_lo[...] = halves(h_ref[...])
    for j in range(8):
        r = slice(128 * j, 128 * j + 128)
        t_hi[r, :], t_lo[r, :] = halves(jnp.transpose(h_ref[:, r]))
    for j in range(4):
        r = slice(256 * j, 256 * j + 256)
        ft = jnp.transpose(f_ref[:, r])
        on = lax.broadcasted_iota(jnp.int32, ft.shape, 0) + 256 * j == lax.broadcasted_iota(jnp.int32, ft.shape, 1)
        gy_hi[r, :], gy_lo[r, :] = halves(product(ft, t_hi, t_lo))
        gp_hi[r, :], gp_lo[r, :] = halves(jnp.where(on, 0.0, ft))
        diag_ref[:, r] = jnp.sum(jnp.where(on, ft, 0.0), axis=0, keepdims=True)[:, r]


def prepare(f, h):
    return pl.pallas_call(
        prepare_kernel,
        out_shape=(
            jax.ShapeDtypeStruct((1024, 1024), BF16),
            jax.ShapeDtypeStruct((1024, 1024), BF16),
            jax.ShapeDtypeStruct((1024, 512), BF16),
            jax.ShapeDtypeStruct((1024, 512), BF16),
            jax.ShapeDtypeStruct((512, 1024), BF16),
            jax.ShapeDtypeStruct((512, 1024), BF16),
            jax.ShapeDtypeStruct((1, 1024), F32),
        ),
        in_specs=[VMEM] * 2,
        out_specs=(VMEM,) * 7,
        scratch_shapes=[pltpu.VMEM((1024, 512), BF16), pltpu.VMEM((1024, 512), BF16)],
        compiler_params=pltpu.CompilerParams(vmem_limit_bytes=32 * 2**20),
        cost_estimate=pl.CostEstimate(flops=3 * 2**30, bytes_accessed=14 * 2**20, transcendentals=0),
        name="prepare",
    )(f, h)


def flat(rows):
    return jnp.concatenate([rows[q : q + 1] for q in range(4)], 1)


def block_kernel(
    at_ref, got0, got1, got2, got3, f_ref, h_ref, s_ref, weight_ref, gp_hi, gp_lo, gy_hi, gy_lo, h_hi, h_lo, diag_ref,
    x_own, x_end, maps, map_ends, state, bits_ref, hw_ref, got_ref,
):
    second, own, plane, place = at_ref[0], at_ref[1], at_ref[2], at_ref[3]
    for n, part in enumerate((got0, got1, got2, got3)):
        got_ref[pl.ds(32 * ((plane + 4 - n) % 4), 32)] = part[...]

    @pl.when(second == 0)
    def _():
        diff = spread_index()
        maps[...] = jnp.zeros_like(maps)
        map_ends[...] = jnp.zeros_like(map_ends)
        store_weighted(hw_ref, h_ref, weight_ref[...], diff)

        def group(g, x):
            words = sum(got_ref[16 * g + j][4:8] * float(2**j) for j in range(16))
            store_bits(bits_ref, words, diff)

            def step(j, x):
                k = 16 * g + j

                @pl.when(k == own)
                def _():
                    x_own[...] = x

                p = propagate(f_ref, x, diff)
                return update(h_ref, hw_ref, bits_ref, jnp.int32(1) << j, got_ref[k][0:4], p, diff)

            return lax.fori_loop(0, 16, step, x)

        x_end[...] = lax.fori_loop(0, 8, group, s_ref[...])

    @pl.when(second == 1)
    def _():
        x_own[...] = jnp.zeros_like(x_own)
        x_end[...] = jnp.zeros_like(x_end)
        unit = (
            lax.broadcasted_iota(jnp.int32, (32, 1024), 1)
            == lax.broadcasted_iota(jnp.int32, (32, 1024), 0) + 32 * place
        ).astype(F32)
        state[0:32, :] = unit
        state[32:64, :] = unit
        state[64:72, :] = jnp.zeros((8, 1024), F32)
        row = lax.broadcasted_iota(jnp.int32, (8, 512), 0)
        weight = flat(weight_ref[...])

        def step(k, carry):
            @pl.when(jnp.logical_and(k // 32 == plane % 2, k % 4 == 0))
            def _():
                q = (k % 32) // 4
                early = plane < 2
                maps[q, 0:32, :] = jnp.where(early, state[0:32, :], state[32:64, :])
                maps[q, 32:40, :] = jnp.where(early, state[64:72, :], pltpu.roll(state[64:72, :], 7, 0))

            x = state[...]
            y = product(x, gy_hi, gy_lo)
            p = product(x, gp_hi, gp_lo) + x * diag_ref[...]
            a, b = got_ref[k], got_ref[64 + k]
            wa, wb = flat(a[4:8]) * weight, flat(b[4:8]) * weight
            zs = jnp.where(row == 0, flat(a[0:4]), jnp.where(row == 1, flat(b[0:4]), 0.0))
            v = jnp.concatenate(
                [
                    -wa * y[0:32],
                    -wb * y[32:64],
                    jnp.where(row == 0, wa, wb) * (zs - y[64:72]),
                ],
                0,
            )
            state[...] = p + product(v, h_hi, h_lo)
            return carry

        lax.fori_loop(0, 64, step, 0)
        map_ends[0:32, :] = state[0:32, :]
        map_ends[32:40, :] = state[64:72, :]


def run_blocks(*args):
    return pl.pallas_call(
        block_kernel,
        out_shape=(
            jax.ShapeDtypeStruct((8, 128), F32),
            jax.ShapeDtypeStruct((8, 128), F32),
            jax.ShapeDtypeStruct((8, 40, 1024), F32),
            jax.ShapeDtypeStruct((40, 1024), F32),
        ),
        in_specs=[SMEM] + [VMEM] * 15,
        out_specs=(VMEM,) * 4,
        scratch_shapes=[pltpu.VMEM((72, 1024), F32), pltpu.VMEM((512, 128), jnp.int32), pltpu.VMEM((512, 1024), F32), pltpu.VMEM((128, 8, 128), F32)],
        compiler_params=pltpu.CompilerParams(vmem_limit_bytes=28 * 2**20),
        name="blocks",
    )(*args)


def own_kernel(z_ref, m_ref, f_ref, h_ref, weight_ref, s_ref, x_out, f_out, bits_ref, hw_ref):
    diff = spread_index()
    store_weighted(hw_ref, h_ref, weight_ref[...], diff)
    store_bits(bits_ref, sum(m_ref[j] * float(2**j) for j in range(4)), diff)

    def step(k, x):
        p = propagate(f_ref, x, diff)

        @pl.when(k > 0)
        def _():
            f_out[k - 1] = p

        x = update(h_ref, hw_ref, bits_ref, jnp.int32(1) << k, z_ref[k], p, diff)
        x_out[k] = x
        return x

    x = lax.fori_loop(0, 4, step, s_ref[...])
    f_out[3] = propagate(f_ref, x, diff)


def run_own(*args):
    return pl.pallas_call(
        own_kernel,
        out_shape=(jax.ShapeDtypeStruct((4, 8, 128), F32),) * 2,
        in_specs=[VMEM] * 6,
        out_specs=(VMEM, VMEM),
        scratch_shapes=[pltpu.VMEM((512, 128), jnp.int32), pltpu.VMEM((512, 1024), F32)],
        compiler_params=pltpu.CompilerParams(vmem_limit_bytes=16 * 2**20),
        name="own_steps",
    )(*args)


def smooth_kernel(at_ref, parts_ref, d_ref, x_ref, f_ref, out_ref):
    at = at_ref[0]
    later = f_ref[3]
    count = parts_ref.shape[0]

    def one(i, later):
        j = count - 1 - i
        e = parts_ref[j]
        return jnp.where(j > at, e[0:2] * later + e[2:4], later)

    later = lax.fori_loop(0, count, one, later)
    for j in reversed(range(4)):
        later = x_ref[j] + d_ref[j] * (later - f_ref[j])
        out_ref[j] = later


def body(z, mask, f, h, weight, d, prior):
    h_at, l_at = lax.axis_index("h"), lax.axis_index("l")
    at = lax.axis_index(TIME)
    place = lax.axis_index(PLANE)
    y = lax.axis_index("y")
    z = z.reshape(4, 4, 128)
    mask = mask.astype(F32).reshape(4, 4, 128)
    own = lax.dynamic_index_in_dim(jnp.concatenate([z, mask], 1), y, 0, True)
    flat_plane = lax.all_to_all(jnp.broadcast_to(own, (32, 8, 128)), PLANE, 0, 0, tiled=True)
    turned = [flat_plane] + [lax.ppermute(flat_plane, "l", [(i, (i + n) % 4) for i in range(4)]) for n in (1, 2, 3)]
    gp_hi, gp_lo, gy_hi, gy_lo, h_hi, h_lo, diag = prepare(f, h)
    weight = weight.reshape(4, 128)
    flags = jnp.stack([h_at, 4 * (at % 32), l_at, place]).astype(jnp.int32)
    x_own, x_end, maps, ends = run_blocks(
        flags, *turned, f, h, prior.reshape(8, 128), weight, gp_hi, gp_lo, gy_hi, gy_lo, h_hi, h_lo, diag
    )
    first = place == 0
    s1 = lax.ppermute(x_end, "h", [(0, 1)]).reshape(32, 32)
    mine = lax.dynamic_index_in_dim(s1, place, 0, False)
    part = jnp.sum(mine[:, None] * ends[:32], 0) + jnp.where(first, ends[32], 0.0)
    s2 = lax.all_to_all(part.reshape(32, 32), PLANE, 0, 0, tiled=True).sum(0)
    mine = jnp.where(l_at < 2, mine, s2)
    parts = jnp.sum(mine[None, :, None] * maps[:, :32], 1) + jnp.where(first, maps[:, 32], 0.0)
    parts = jnp.broadcast_to(parts[:, None], (8, 4, 1024)).reshape(32, 1024)
    begin = lax.all_to_all(parts, PLANE, 0, 0, tiled=True).sum(0).reshape(8, 128)
    begin = jnp.where(h_at == 0, x_own, begin)
    x4, f4 = run_own(z, mask, f, h, weight, begin)
    x4 = lax.dynamic_slice_in_dim(x4, 2 * y, 2, 1)
    f4 = lax.dynamic_slice_in_dim(f4, 2 * y, 2, 1)
    d4 = d.reshape(4, 2, 128)
    last = at == 63
    factor = jnp.ones((2, 128), F32)
    const = jnp.where(last, f4[3], 0.0)
    for j in reversed(range(4)):
        const = x4[j] + d4[j] * (const - f4[j])
        factor = factor * d4[j]
    element = jnp.concatenate([jnp.where(last, 0.0, factor), const], 0)
    parts = lax.all_to_all(jnp.broadcast_to(element[None], (64, 4, 128)), TIME, 0, 0, tiled=True)
    smooth = pl.pallas_call(
        smooth_kernel,
        out_shape=jax.ShapeDtypeStruct((4, 2, 128), F32),
        in_specs=[SMEM] + [VMEM] * 4,
        out_specs=VMEM,
        name="smooth_own",
    )(at.reshape(1), parts, d4, x4, f4)
    return x4.reshape(4, 256), smooth.reshape(4, 256)


def solution(mesh):
    fine = Mesh(mesh.devices.reshape(2, 4, 4, 2, 4), TIME + ("y",))
    t = P(TIME, None)
    ty = P(TIME, "y")
    return jax.shard_map(
        body,
        mesh=fine,
        in_specs=(t, t, P(), P(), P(), ty, P()),
        out_specs=(ty, ty),
        check_vma=False,
    )
```

```python
import functools

import jax
import jax.numpy as jnp
from jax import lax
from jax.experimental import pallas as pl
from jax.experimental.pallas import tpu as pltpu
from jax.sharding import Mesh, PartitionSpec as P

F32 = jnp.float32
HALF = ("l", "x", "c", "y")
PLANE = ("x", "c", "y")
TIME = ("h", "l", "x", "c")
BF16 = jnp.bfloat16
VMEM = pl.BlockSpec(memory_space=pltpu.VMEM)
SMEM = pl.BlockSpec(memory_space=pltpu.SMEM)


def wide(row):
    return jnp.broadcast_to(row, (8, 128))


def tree(terms):
    while len(terms) > 1:
        terms = [a + b for a, b in zip(terms[::2], terms[1::2])]
    return terms[0]


def column_sums(blocks):
    return jnp.concatenate([jnp.sum(b, axis=0, keepdims=True) for b in blocks], 0)


def propagate(f_ref, x, diff):
    xs = [wide(x[t : t + 1]) for t in range(8)]
    out = []
    for t in range(8):
        spread = None
        for b in range(16):
            i = 8 * (16 * t + b)
            s = tree([f_ref[i : i + 8, 128 * u : 128 * u + 128] * xs[u] for u in range(8)])
            s = wide(jnp.sum(s, axis=1, keepdims=True))
            spread = jnp.where(diff == 8 * b, s, 0.0 if spread is None else spread)
        out.append(spread)
    return column_sums(out)


def update(h_ref, hw_ref, bits_ref, bit, z, p, diff):
    ps = [wide(p[t : t + 1]) for t in range(8)]
    zs = [wide(z[q : q + 1]) for q in range(4)]
    acc = [jnp.zeros((8, 128), F32) for _ in range(8)]
    for i in range(64):
        r = slice(8 * i, 8 * i + 8)
        s = tree([h_ref[r, 128 * t : 128 * t + 128] * ps[t] for t in range(8)])
        s = jnp.where(diff == 8 * (i % 16), zs[i // 16], 0.0) - s
        s = wide(jnp.sum(s, axis=1, keepdims=True))
        v = jnp.where((bits_ref[r, :] & bit) != 0, s, 0.0)
        acc = [acc[t] + hw_ref[r, 128 * t : 128 * t + 128] * v for t in range(8)]
    return p + column_sums(acc)


def spread_index():
    return lax.broadcasted_iota(jnp.int32, (8, 128), 1) - lax.broadcasted_iota(jnp.int32, (8, 128), 0)


def halves(x):
    hi = x.astype(BF16)
    return hi, (x - hi.astype(F32)).astype(BF16)


def product(x, hi_ref, lo_ref):
    n = x.shape[0]
    hi, lo = halves(x)
    both = jnp.dot(jnp.concatenate([hi, lo], 0), hi_ref[...], preferred_element_type=F32)
    return both[:n] + both[n:] + jnp.dot(hi, lo_ref[...], preferred_element_type=F32)


def on_rows(words, i, diff):
    q = i // 16
    return wide(jnp.sum(jnp.where(diff == 8 * (i % 16), wide(words[q : q + 1]), 0.0), axis=1, keepdims=True))


def store_bits(bits_ref, words, diff):
    for i in range(64):
        bits_ref[8 * i : 8 * i + 8, :] = on_rows(words, i, diff).astype(jnp.int32)


def store_weighted(hw_ref, h_ref, weight, diff):
    for i in range(64):
        r = slice(8 * i, 8 * i + 8)
        w = on_rows(weight, i, diff)
        for t in range(8):
            c = slice(128 * t, 128 * t + 128)
            hw_ref[r, c] = h_ref[r, c] * w


def prepare(f_ref, h_ref, gp_hi, gp_lo, gy_hi, gy_lo, h_hi, h_lo, diag_ref, t_hi, t_lo):
    h_hi[...], h_lo[...] = halves(h_ref[...])
    for j in range(8):
        r = slice(128 * j, 128 * j + 128)
        t_hi[r, :], t_lo[r, :] = halves(jnp.transpose(h_ref[:, r]))
    for j in range(4):
        r = slice(256 * j, 256 * j + 256)
        ft = jnp.transpose(f_ref[:, r])
        row = lax.broadcasted_iota(jnp.int32, ft.shape, 0) + 256 * j
        on = row == lax.broadcasted_iota(jnp.int32, ft.shape, 1)
        gy_hi[r, :], gy_lo[r, :] = halves(product(ft, t_hi, t_lo))
        gp_hi[r, :], gp_lo[r, :] = halves(jnp.where(on, 0.0, ft))
        diag_ref[:, r] = jnp.sum(jnp.where(on, ft, 0.0), axis=0, keepdims=True)[:, r]


def flat(rows):
    return jnp.concatenate([rows[q : q + 1] for q in range(4)], 1)


def block_kernel(
    at_ref, got0, got1, got2, got3, f_ref, h_ref, s_ref, weight_ref,
    x_own, x_end, maps, map_ends, state, bits_ref, hw_ref, got_ref,
    gp_hi, gp_lo, gy_hi, gy_lo, h_hi, h_lo, diag_ref, t_hi, t_lo,
):
    second, own, plane, place = at_ref[0], at_ref[1], at_ref[2], at_ref[3]
    for n, part in enumerate((got0, got1, got2, got3)):
        got_ref[pl.ds(32 * ((plane + 4 - n) % 4), 32)] = part[...]

    @pl.when(second == 0)
    def _():
        diff = spread_index()
        maps[...] = jnp.zeros_like(maps)
        map_ends[...] = jnp.zeros_like(map_ends)
        store_weighted(hw_ref, h_ref, weight_ref[...], diff)

        def group(g, x):
            words = sum(got_ref[16 * g + j][4:8] * float(2**j) for j in range(16))
            store_bits(bits_ref, words, diff)

            def step(j, x):
                k = 16 * g + j

                @pl.when(k == own)
                def _():
                    x_own[...] = x

                p = propagate(f_ref, x, diff)
                return update(h_ref, hw_ref, bits_ref, jnp.int32(1) << j, got_ref[k][0:4], p, diff)

            return lax.fori_loop(0, 16, step, x)

        x_end[...] = lax.fori_loop(0, 8, group, s_ref[...])

    @pl.when(second == 1)
    def _():
        x_own[...] = jnp.zeros_like(x_own)
        x_end[...] = jnp.zeros_like(x_end)
        prepare(f_ref, h_ref, gp_hi, gp_lo, gy_hi, gy_lo, h_hi, h_lo, diag_ref, t_hi, t_lo)
        unit = (
            lax.broadcasted_iota(jnp.int32, (32, 1024), 1)
            == lax.broadcasted_iota(jnp.int32, (32, 1024), 0) + 32 * place
        ).astype(F32)
        state[0:32, :] = unit
        state[32:64, :] = unit
        state[64:72, :] = jnp.zeros((8, 1024), F32)
        row = lax.broadcasted_iota(jnp.int32, (8, 512), 0)
        weight = flat(weight_ref[...])

        def step(k, carry):
            @pl.when(jnp.logical_and(k // 32 == plane % 2, k % 4 == 0))
            def _():
                q = (k % 32) // 4
                early = plane < 2
                maps[q, 0:32, :] = jnp.where(early, state[0:32, :], state[32:64, :])
                maps[q, 32:40, :] = jnp.where(early, state[64:72, :], pltpu.roll(state[64:72, :], 7, 0))

            x = state[...]
            y = product(x, gy_hi, gy_lo)
            p = product(x, gp_hi, gp_lo) + x * diag_ref[...]
            a, b = got_ref[k], got_ref[64 + k]
            wa, wb = flat(a[4:8]) * weight, flat(b[4:8]) * weight
            zs = jnp.where(row == 0, flat(a[0:4]), jnp.where(row == 1, flat(b[0:4]), 0.0))
            v = jnp.concatenate(
                [
                    -wa * y[0:32],
                    -wb * y[32:64],
                    jnp.where(row == 0, wa, wb) * (zs - y[64:72]),
                ],
                0,
            )
            state[...] = p + product(v, h_hi, h_lo)
            return carry

        lax.fori_loop(0, 64, step, 0)
        map_ends[0:32, :] = state[0:32, :]
        map_ends[32:40, :] = state[64:72, :]


def run_blocks(*args):
    return pl.pallas_call(
        block_kernel,
        out_shape=(
            jax.ShapeDtypeStruct((8, 128), F32),
            jax.ShapeDtypeStruct((8, 128), F32),
            jax.ShapeDtypeStruct((8, 40, 1024), F32),
            jax.ShapeDtypeStruct((40, 1024), F32),
        ),
        in_specs=[SMEM] + [VMEM] * 8,
        out_specs=(VMEM,) * 4,
        scratch_shapes=[
            pltpu.VMEM((72, 1024), F32),
            pltpu.VMEM((512, 128), jnp.int32),
            pltpu.VMEM((512, 1024), F32),
            pltpu.VMEM((128, 8, 128), F32),
            *[pltpu.VMEM((1024, 1024), BF16)] * 2,
            *[pltpu.VMEM((1024, 512), BF16)] * 2,
            *[pltpu.VMEM((512, 1024), BF16)] * 2,
            pltpu.VMEM((1, 1024), F32),
            *[pltpu.VMEM((1024, 512), BF16)] * 2,
        ],
        compiler_params=pltpu.CompilerParams(vmem_limit_bytes=36 * 2**20),
        name="blocks",
    )(*args)


def parts_kernel(at_ref, s1_ref, s2_ref, maps_ref, out_ref):
    s2 = jnp.sum(s2_ref[...], axis=0, keepdims=True)
    s = jnp.where(at_ref[2] < 2, s1_ref[...], s2)
    s = jnp.broadcast_to(s, (32, 32))
    on = lax.broadcasted_iota(jnp.int32, (32, 32), 0) == lax.broadcasted_iota(jnp.int32, (32, 32), 1)
    s = jnp.sum(jnp.where(on, s, 0.0), axis=1, keepdims=True)
    once = (at_ref[3] == 0).astype(F32)
    for q in range(8):
        total = jnp.sum(s * maps_ref[q, 0:32, :], axis=0, keepdims=True) + once * maps_ref[q, 32:33, :]
        for j in range(4):
            for t in range(8):
                out_ref[4 * q + j, t : t + 1, :] = total[:, 128 * t : 128 * t + 128]


def run_parts(*args):
    return pl.pallas_call(
        parts_kernel,
        out_shape=jax.ShapeDtypeStruct((32, 8, 128), F32),
        in_specs=[SMEM] + [VMEM] * 3,
        out_specs=VMEM,
        name="parts",
    )(*args)


def own_kernel(
    at_ref, z_ref, m_ref, f_ref, h_ref, weight_ref, d_ref, x_own, got_ref,
    x_out, f_out, e_out, bits_ref, hw_ref, xs, fs,
):
    diff = spread_index()
    store_weighted(hw_ref, h_ref, weight_ref[...], diff)
    store_bits(bits_ref, sum(m_ref[j] * float(2**j) for j in range(4)), diff)

    def step(k, x):
        p = propagate(f_ref, x, diff)

        @pl.when(k > 0)
        def _():
            fs[k - 1] = p

        x = update(h_ref, hw_ref, bits_ref, jnp.int32(1) << k, z_ref[k], p, diff)
        xs[k] = x
        return x

    begin = jnp.where(at_ref[0] == 0, x_own[...], jnp.sum(got_ref[...], axis=0))
    x = lax.fori_loop(0, 4, step, begin)
    fs[3] = propagate(f_ref, x, diff)
    shift = (8 - 2 * at_ref[4]) % 8
    x4 = [pltpu.roll(xs[j], shift, 0)[0:2] for j in range(4)]
    f4 = [pltpu.roll(fs[j], shift, 0)[0:2] for j in range(4)]
    last = at_ref[5] == 63
    factor = jnp.ones((2, 128), F32)
    const = jnp.where(last, f4[3], 0.0)
    for j in reversed(range(4)):
        const = x4[j] + d_ref[j] * (const - f4[j])
        factor = factor * d_ref[j]
        x_out[j] = x4[j]
        f_out[j] = f4[j]
    element = jnp.concatenate([jnp.where(last, 0.0, factor), const], 0)
    e_out[...] = jnp.broadcast_to(element[None], e_out.shape)


def run_own(*args):
    return pl.pallas_call(
        own_kernel,
        out_shape=(
            jax.ShapeDtypeStruct((4, 2, 128), F32),
            jax.ShapeDtypeStruct((4, 2, 128), F32),
            jax.ShapeDtypeStruct((64, 4, 128), F32),
        ),
        in_specs=[SMEM] + [VMEM] * 8,
        out_specs=(VMEM,) * 3,
        scratch_shapes=[
            pltpu.VMEM((512, 128), jnp.int32),
            pltpu.VMEM((512, 1024), F32),
            pltpu.VMEM((4, 8, 128), F32),
            pltpu.VMEM((4, 8, 128), F32),
        ],
        compiler_params=pltpu.CompilerParams(vmem_limit_bytes=20 * 2**20),
        name="own_steps",
    )(*args)


def smooth_kernel(at_ref, parts_ref, d_ref, x_ref, f_ref, x_out, r_out):
    at = at_ref[5]
    later = f_ref[3]
    count = parts_ref.shape[0]

    def one(i, later):
        j = count - 1 - i
        e = parts_ref[j]
        return jnp.where(j > at, e[0:2] * later + e[2:4], later)

    later = lax.fori_loop(0, count, one, later)
    for j in reversed(range(4)):
        x = x_ref[j]
        later = x + d_ref[j] * (later - f_ref[j])
        for q in range(2):
            x_out[j : j + 1, 128 * q : 128 * q + 128] = x[q : q + 1]
            r_out[j : j + 1, 128 * q : 128 * q + 128] = later[q : q + 1]


def run_smooth(*args):
    return pl.pallas_call(
        smooth_kernel,
        out_shape=(jax.ShapeDtypeStruct((4, 256), F32),) * 2,
        in_specs=[SMEM] + [VMEM] * 4,
        out_specs=(VMEM, VMEM),
        name="smooth_own",
    )(*args)


def body(z, mask, f, h, weight, d, prior):
    h_at, l_at = lax.axis_index("h"), lax.axis_index("l")
    at = lax.axis_index(TIME)
    place = lax.axis_index(PLANE)
    y = lax.axis_index("y")
    flags = jnp.stack([h_at, 4 * (at % 32), l_at, place, y, at]).astype(jnp.int32)
    own_z = lax.dynamic_slice_in_dim(z, y, 1, 0).reshape(4, 128)
    own_m = lax.dynamic_slice_in_dim(mask, y, 1, 0).astype(F32).reshape(4, 128)
    own = jnp.broadcast_to(jnp.concatenate([own_z, own_m], 0)[None], (32, 8, 128))
    got = lax.all_to_all(own, PLANE, 0, 0, tiled=True)
    turned = [got] + [lax.ppermute(got, "l", [(i, (i + n) % 4) for i in range(4)]) for n in (1, 2, 3)]
    weight = weight.reshape(4, 128)
    x_own, x_end, maps, ends = run_blocks(flags, *turned, f, h, prior.reshape(8, 128), weight)
    s1 = lax.ppermute(x_end, "h", [(0, 1)]).reshape(32, 32)
    s1 = lax.dynamic_slice_in_dim(s1, place, 1, 0)
    part = jnp.sum(s1.reshape(32, 1) * ends[:32], 0) + jnp.where(place == 0, ends[32], 0.0)
    s2 = lax.all_to_all(part.reshape(32, 32), PLANE, 0, 0, tiled=True)
    parts = lax.all_to_all(run_parts(flags, s1, s2, maps), PLANE, 0, 0, tiled=True)
    z4 = z.reshape(4, 4, 128)
    m4 = mask.astype(F32).reshape(4, 4, 128)
    d4 = d.reshape(4, 2, 128)
    x4, f4, element = run_own(flags, z4, m4, f, h, weight, d4, x_own, parts)
    elements = lax.all_to_all(element, TIME, 0, 0, tiled=True)
    return run_smooth(flags, elements, d4, x4, f4)


def solution(mesh):
    fine = Mesh(mesh.devices.reshape(2, 4, 4, 2, 4), TIME + ("y",))
    t = P(TIME, None)
    ty = P(TIME, "y")
    return jax.shard_map(
        body,
        mesh=fine,
        in_specs=(t, t, P(), P(), P(), ty, P()),
        out_specs=(ty, ty),
        check_vma=False,
    )
```

```python
import functools

import jax
import jax.numpy as jnp
from jax import lax
from jax.experimental import pallas as pl
from jax.experimental.pallas import tpu as pltpu
from jax.sharding import Mesh, PartitionSpec as P

F32 = jnp.float32
HALF = ("l", "x", "c", "y")
PLANE = ("x", "c", "y")
TIME = ("h", "l", "x", "c")
BF16 = jnp.bfloat16
VMEM = pl.BlockSpec(memory_space=pltpu.VMEM)
SMEM = pl.BlockSpec(memory_space=pltpu.SMEM)
ANY = pl.BlockSpec(memory_space=pl.ANY)


def wide(row):
    return jnp.broadcast_to(row, (8, 128))


def tree(terms):
    while len(terms) > 1:
        terms = [a + b for a, b in zip(terms[::2], terms[1::2])]
    return terms[0]


def column_sums(blocks):
    return jnp.concatenate([jnp.sum(b, axis=0, keepdims=True) for b in blocks], 0)


def propagate(f_ref, x, diff):
    xs = [wide(x[t : t + 1]) for t in range(8)]
    out = []
    for t in range(8):
        spread = None
        for b in range(16):
            i = 8 * (16 * t + b)
            s = tree([f_ref[i : i + 8, 128 * u : 128 * u + 128] * xs[u] for u in range(8)])
            s = wide(jnp.sum(s, axis=1, keepdims=True))
            spread = jnp.where(diff == 8 * b, s, 0.0 if spread is None else spread)
        out.append(spread)
    return column_sums(out)


def update(h_ref, hw_ref, bits_ref, bit, z, p, diff):
    ps = [wide(p[t : t + 1]) for t in range(8)]
    zs = [wide(z[q : q + 1]) for q in range(4)]
    acc = [jnp.zeros((8, 128), F32) for _ in range(8)]
    for i in range(64):
        r = slice(8 * i, 8 * i + 8)
        s = tree([h_ref[r, 128 * t : 128 * t + 128] * ps[t] for t in range(8)])
        s = jnp.where(diff == 8 * (i % 16), zs[i // 16], 0.0) - s
        s = wide(jnp.sum(s, axis=1, keepdims=True))
        v = jnp.where((bits_ref[r, :] & bit) != 0, s, 0.0)
        acc = [acc[t] + hw_ref[r, 128 * t : 128 * t + 128] * v for t in range(8)]
    return p + column_sums(acc)


def spread_index():
    return lax.broadcasted_iota(jnp.int32, (8, 128), 1) - lax.broadcasted_iota(jnp.int32, (8, 128), 0)


def halves(x):
    hi = x.astype(BF16)
    return hi, (x - hi.astype(F32)).astype(BF16)


def product(x, hi_ref, lo_ref):
    n = x.shape[0]
    hi, lo = halves(x)
    both = jnp.dot(jnp.concatenate([hi, lo], 0), hi_ref[...], preferred_element_type=F32)
    return both[:n] + both[n:] + jnp.dot(hi, lo_ref[...], preferred_element_type=F32)


def on_rows(words, i, diff):
    q = i // 16
    return wide(jnp.sum(jnp.where(diff == 8 * (i % 16), wide(words[q : q + 1]), 0.0), axis=1, keepdims=True))


def store_bits(bits_ref, words, diff):
    for i in range(64):
        bits_ref[8 * i : 8 * i + 8, :] = on_rows(words, i, diff).astype(jnp.int32)


def store_weighted(hw_ref, h_ref, weight, diff):
    for i in range(64):
        r = slice(8 * i, 8 * i + 8)
        w = on_rows(weight, i, diff)
        for t in range(8):
            c = slice(128 * t, 128 * t + 128)
            hw_ref[r, c] = h_ref[r, c] * w


def prepare_kernel(f_ref, h_ref, gp_hi, gp_lo, gy_hi, gy_lo, h_hi, h_lo, diag_ref, t_hi, t_lo):
    h_hi[...], h_lo[...] = halves(h_ref[...])
    for j in range(8):
        r = slice(128 * j, 128 * j + 128)
        t_hi[r, :], t_lo[r, :] = halves(jnp.transpose(h_ref[:, r]))
    for j in range(4):
        r = slice(256 * j, 256 * j + 256)
        ft = jnp.transpose(f_ref[:, r])
        row = lax.broadcasted_iota(jnp.int32, ft.shape, 0) + 256 * j
        on = row == lax.broadcasted_iota(jnp.int32, ft.shape, 1)
        gy_hi[r, :], gy_lo[r, :] = halves(product(ft, t_hi, t_lo))
        gp_hi[r, :], gp_lo[r, :] = halves(jnp.where(on, 0.0, ft))
        diag_ref[:, r] = jnp.sum(jnp.where(on, ft, 0.0), axis=0, keepdims=True)[:, r]


def prepare(f, h):
    return pl.pallas_call(
        prepare_kernel,
        out_shape=(
            *[jax.ShapeDtypeStruct((1024, 1024), BF16)] * 2,
            *[jax.ShapeDtypeStruct((1024, 512), BF16)] * 2,
            *[jax.ShapeDtypeStruct((512, 1024), BF16)] * 2,
            jax.ShapeDtypeStruct((1, 1024), F32),
        ),
        in_specs=[VMEM] * 2,
        out_specs=(VMEM,) * 7,
        scratch_shapes=[pltpu.VMEM((1024, 512), BF16)] * 2,
        compiler_params=pltpu.CompilerParams(vmem_limit_bytes=26 * 2**20),
        cost_estimate=pl.CostEstimate(flops=3 * 2**30, bytes_accessed=14 * 2**20, transcendentals=0),
        name="prepare",
    )(f, h)


def flat(rows):
    return jnp.concatenate([rows[q : q + 1] for q in range(4)], 1)


def block_kernel(
    at_ref, got_ref, s_ref, weight_ref, diag_ref, f_any, h_any, *rest,
):
    mats_any, (x_own, x_end, maps, map_ends), rest = rest[:6], rest[6:10], rest[10:]
    state, bits_ref, hw_ref, f_ref, h_ref, *mats, sems = rest
    gp_hi, gp_lo, gy_hi, gy_lo, h_hi, h_lo = mats
    second, own, plane, place = at_ref[0], at_ref[1], at_ref[2], at_ref[3]

    def fetch(pairs):
        copies = [pltpu.make_async_copy(a, b, sems.at[i]) for i, (a, b) in enumerate(pairs)]
        for c in copies:
            c.start()
        for c in copies:
            c.wait()

    def at_step(k):
        return got_ref[k % 32, (plane + 4 - k // 32) % 4]


    @pl.when(second == 0)
    def _():
        fetch([(f_any, f_ref), (h_any, h_ref)])
        diff = spread_index()
        maps[...] = jnp.zeros_like(maps)
        map_ends[...] = jnp.zeros_like(map_ends)
        store_weighted(hw_ref, h_ref, weight_ref[...], diff)

        def group(g, x):
            words = sum(at_step(16 * g + j)[4:8] * float(2**j) for j in range(16))
            store_bits(bits_ref, words, diff)

            def step(j, x):
                k = 16 * g + j

                @pl.when(k == own)
                def _():
                    x_own[...] = x

                p = propagate(f_ref, x, diff)
                return update(h_ref, hw_ref, bits_ref, jnp.int32(1) << j, at_step(k)[0:4], p, diff)

            return lax.fori_loop(0, 16, step, x)

        x_end[...] = lax.fori_loop(0, 8, group, s_ref[...])

    @pl.when(second == 1)
    def _():
        x_own[...] = jnp.zeros_like(x_own)
        x_end[...] = jnp.zeros_like(x_end)
        fetch(list(zip(mats_any, mats)))
        unit = (
            lax.broadcasted_iota(jnp.int32, (32, 1024), 1)
            == lax.broadcasted_iota(jnp.int32, (32, 1024), 0) + 32 * place
        ).astype(F32)
        state[0:32, :] = unit
        state[32:64, :] = unit
        state[64:72, :] = jnp.zeros((8, 1024), F32)
        row = lax.broadcasted_iota(jnp.int32, (8, 512), 0)
        weight = flat(weight_ref[...])

        def step(k, carry):
            @pl.when(jnp.logical_and(k // 32 == plane % 2, k % 4 == 0))
            def _():
                q = (k % 32) // 4
                early = plane < 2
                maps[q, 0:32, :] = jnp.where(early, state[0:32, :], state[32:64, :])
                maps[q, 32:40, :] = jnp.where(early, state[64:72, :], pltpu.roll(state[64:72, :], 7, 0))

            x = state[...]
            y = product(x, gy_hi, gy_lo)
            p = product(x, gp_hi, gp_lo) + x * diag_ref[...]
            a, b = at_step(k), at_step(64 + k)
            wa, wb = flat(a[4:8]) * weight, flat(b[4:8]) * weight
            zs = jnp.where(row == 0, flat(a[0:4]), jnp.where(row == 1, flat(b[0:4]), 0.0))
            v = jnp.concatenate(
                [
                    -wa * y[0:32],
                    -wb * y[32:64],
                    jnp.where(row == 0, wa, wb) * (zs - y[64:72]),
                ],
                0,
            )
            state[...] = p + product(v, h_hi, h_lo)
            return carry

        lax.fori_loop(0, 64, step, 0)
        map_ends[0:32, :] = state[0:32, :]
        map_ends[32:40, :] = state[64:72, :]


def run_blocks(*args):
    return pl.pallas_call(
        block_kernel,
        out_shape=(
            jax.ShapeDtypeStruct((8, 128), F32),
            jax.ShapeDtypeStruct((8, 128), F32),
            jax.ShapeDtypeStruct((8, 40, 1024), F32),
            jax.ShapeDtypeStruct((40, 1024), F32),
        ),
        in_specs=[SMEM] + [VMEM] * 4 + [ANY] * 8,
        out_specs=(VMEM,) * 4,
        scratch_shapes=[
            pltpu.VMEM((72, 1024), F32),
            pltpu.VMEM((512, 128), jnp.int32),
            pltpu.VMEM((512, 1024), F32),
            pltpu.VMEM((1024, 1024), F32),
            pltpu.VMEM((512, 1024), F32),
            *[pltpu.VMEM((1024, 1024), BF16)] * 2,
            *[pltpu.VMEM((1024, 512), BF16)] * 2,
            *[pltpu.VMEM((512, 1024), BF16)] * 2,
            pltpu.SemaphoreType.DMA((6,)),
        ],
        compiler_params=pltpu.CompilerParams(vmem_limit_bytes=58 * 2**20),
        name="blocks",
    )(*args)


def parts_kernel(at_ref, s1_ref, s2_ref, maps_ref, out_ref):
    s2 = jnp.sum(s2_ref[...], axis=0, keepdims=True)
    s = jnp.where(at_ref[2] < 2, s1_ref[...], s2)
    s = jnp.broadcast_to(s, (32, 32))
    on = lax.broadcasted_iota(jnp.int32, (32, 32), 0) == lax.broadcasted_iota(jnp.int32, (32, 32), 1)
    s = jnp.sum(jnp.where(on, s, 0.0), axis=1, keepdims=True)
    once = (at_ref[3] == 0).astype(F32)
    for q in range(8):
        total = jnp.sum(s * maps_ref[q, 0:32, :], axis=0, keepdims=True) + once * maps_ref[q, 32:33, :]
        for j in range(4):
            for t in range(8):
                out_ref[4 * q + j, t : t + 1, :] = total[:, 128 * t : 128 * t + 128]


def run_parts(*args):
    return pl.pallas_call(
        parts_kernel,
        out_shape=jax.ShapeDtypeStruct((32, 8, 128), F32),
        in_specs=[SMEM] + [VMEM] * 3,
        out_specs=VMEM,
        compiler_params=pltpu.CompilerParams(vmem_limit_bytes=6 * 2**20),
        name="parts",
    )(*args)


def own_kernel(
    at_ref, z_ref, m_ref, f_ref, h_ref, weight_ref, d_ref, x_own, got_ref,
    x_out, f_out, e_out, bits_ref, hw_ref, xs, fs,
):
    diff = spread_index()
    store_weighted(hw_ref, h_ref, weight_ref[...], diff)
    store_bits(bits_ref, sum(m_ref[j] * float(2**j) for j in range(4)), diff)

    def step(k, x):
        p = propagate(f_ref, x, diff)

        @pl.when(k > 0)
        def _():
            fs[k - 1] = p

        x = update(h_ref, hw_ref, bits_ref, jnp.int32(1) << k, z_ref[k], p, diff)
        xs[k] = x
        return x

    begin = jnp.where(at_ref[0] == 0, x_own[...], jnp.sum(got_ref[...], axis=0))
    x = lax.fori_loop(0, 4, step, begin)
    fs[3] = propagate(f_ref, x, diff)
    shift = (8 - 2 * at_ref[4]) % 8
    x4 = [pltpu.roll(xs[j], shift, 0)[0:2] for j in range(4)]
    f4 = [pltpu.roll(fs[j], shift, 0)[0:2] for j in range(4)]
    last = at_ref[5] == 63
    factor = jnp.ones((2, 128), F32)
    const = jnp.where(last, f4[3], 0.0)
    for j in reversed(range(4)):
        const = x4[j] + d_ref[j] * (const - f4[j])
        factor = factor * d_ref[j]
        x_out[j] = x4[j]
        f_out[j] = f4[j]
    element = jnp.concatenate([jnp.where(last, 0.0, factor), const], 0)
    e_out[...] = jnp.broadcast_to(element[None], e_out.shape)


def run_own(*args):
    return pl.pallas_call(
        own_kernel,
        out_shape=(
            jax.ShapeDtypeStruct((4, 2, 128), F32),
            jax.ShapeDtypeStruct((4, 2, 128), F32),
            jax.ShapeDtypeStruct((64, 4, 128), F32),
        ),
        in_specs=[SMEM] + [VMEM] * 8,
        out_specs=(VMEM,) * 3,
        scratch_shapes=[
            pltpu.VMEM((512, 128), jnp.int32),
            pltpu.VMEM((512, 1024), F32),
            pltpu.VMEM((4, 8, 128), F32),
            pltpu.VMEM((4, 8, 128), F32),
        ],
        compiler_params=pltpu.CompilerParams(vmem_limit_bytes=12 * 2**20),
        name="own_steps",
    )(*args)


def smooth_kernel(at_ref, parts_ref, d_ref, x_ref, f_ref, x_out, r_out):
    at = at_ref[5]
    later = f_ref[3]
    count = parts_ref.shape[0]

    def one(i, later):
        j = count - 1 - i
        e = parts_ref[j]
        return jnp.where(j > at, e[0:2] * later + e[2:4], later)

    later = lax.fori_loop(0, count, one, later)
    for j in reversed(range(4)):
        x = x_ref[j]
        later = x + d_ref[j] * (later - f_ref[j])
        for q in range(2):
            x_out[j : j + 1, 128 * q : 128 * q + 128] = x[q : q + 1]
            r_out[j : j + 1, 128 * q : 128 * q + 128] = later[q : q + 1]


def run_smooth(*args):
    return pl.pallas_call(
        smooth_kernel,
        out_shape=(jax.ShapeDtypeStruct((4, 256), F32),) * 2,
        in_specs=[SMEM] + [VMEM] * 4,
        out_specs=(VMEM, VMEM),
        compiler_params=pltpu.CompilerParams(vmem_limit_bytes=4 * 2**20),
        name="smooth_own",
    )(*args)


def body(z, mask, f, h, weight, d, prior):
    h_at, l_at = lax.axis_index("h"), lax.axis_index("l")
    at = lax.axis_index(TIME)
    place = lax.axis_index(PLANE)
    y = lax.axis_index("y")
    flags = jnp.stack([h_at, 4 * (at % 32), l_at, place, y, at]).astype(jnp.int32)
    own_z = lax.dynamic_slice_in_dim(z, y, 1, 0).reshape(4, 128)
    own_m = lax.dynamic_slice_in_dim(mask, y, 1, 0).astype(F32).reshape(4, 128)
    own = jnp.concatenate([own_z, own_m], 0)
    turned = [lax.ppermute(own, "l", [(i, (i + n) % 4) for i in range(4)]) for n in (1, 2, 3)]
    *mats, diag = prepare(f, h)
    own = jnp.broadcast_to(jnp.stack([own, *turned])[None], (32, 4, 8, 128))
    got = lax.all_to_all(own, PLANE, 0, 0, tiled=True)
    weight = weight.reshape(4, 128)
    x_own, x_end, maps, ends = run_blocks(flags, got, prior.reshape(8, 128), weight, diag, f, h, *mats)
    s1 = lax.ppermute(x_end, "h", [(0, 1)]).reshape(32, 32)
    s1 = lax.dynamic_slice_in_dim(s1, place, 1, 0)
    part = jnp.sum(s1.reshape(32, 1) * ends[:32], 0) + jnp.where(place == 0, ends[32], 0.0)
    s2 = lax.all_to_all(part.reshape(32, 32), PLANE, 0, 0, tiled=True)
    parts = lax.all_to_all(run_parts(flags, s1, s2, maps), PLANE, 0, 0, tiled=True)
    z4 = z.reshape(4, 4, 128)
    m4 = mask.astype(F32).reshape(4, 4, 128)
    d4 = d.reshape(4, 2, 128)
    x4, f4, element = run_own(flags, z4, m4, f, h, weight, d4, x_own, parts)
    elements = lax.all_to_all(element, TIME, 0, 0, tiled=True)
    return run_smooth(flags, elements, d4, x4, f4)


def solution(mesh):
    fine = Mesh(mesh.devices.reshape(2, 4, 4, 2, 4), TIME + ("y",))
    t = P(TIME, None)
    ty = P(TIME, "y")
    return jax.shard_map(
        body,
        mesh=fine,
        in_specs=(t, t, P(), P(), P(), ty, P()),
        out_specs=(ty, ty),
        check_vma=False,
    )
```

```python
import functools

import jax
import jax.numpy as jnp
from jax import lax
from jax.experimental import pallas as pl
from jax.experimental.pallas import tpu as pltpu
from jax.sharding import Mesh, PartitionSpec as P

F32 = jnp.float32
HALF = ("l", "x", "c", "y")
PLANE = ("x", "c", "y")
TIME = ("h", "l", "x", "c")
BF16 = jnp.bfloat16
VMEM = pl.BlockSpec(memory_space=pltpu.VMEM)
SMEM = pl.BlockSpec(memory_space=pltpu.SMEM)
ANY = pl.BlockSpec(memory_space=pl.ANY)


def wide(row):
    return jnp.broadcast_to(row, (8, 128))


def tree(terms):
    while len(terms) > 1:
        terms = [a + b for a, b in zip(terms[::2], terms[1::2])]
    return terms[0]


def column_sums(blocks):
    return jnp.concatenate([jnp.sum(b, axis=0, keepdims=True) for b in blocks], 0)


def propagate(f_ref, x, diff):
    xs = [wide(x[t : t + 1]) for t in range(8)]
    out = []
    for t in range(8):
        spread = None
        for b in range(16):
            i = 8 * (16 * t + b)
            s = tree([f_ref[i : i + 8, 128 * u : 128 * u + 128] * xs[u] for u in range(8)])
            s = wide(jnp.sum(s, axis=1, keepdims=True))
            spread = jnp.where(diff == 8 * b, s, 0.0 if spread is None else spread)
        out.append(spread)
    return column_sums(out)


def update(h_ref, hw_ref, bits_ref, bit, z, p, diff):
    ps = [wide(p[t : t + 1]) for t in range(8)]
    zs = [wide(z[q : q + 1]) for q in range(4)]
    acc = [jnp.zeros((8, 128), F32) for _ in range(8)]
    for i in range(64):
        r = slice(8 * i, 8 * i + 8)
        s = tree([h_ref[r, 128 * t : 128 * t + 128] * ps[t] for t in range(8)])
        s = jnp.where(diff == 8 * (i % 16), zs[i // 16], 0.0) - s
        s = wide(jnp.sum(s, axis=1, keepdims=True))
        v = jnp.where((bits_ref[r, :] & bit) != 0, s, 0.0)
        acc = [acc[t] + hw_ref[r, 128 * t : 128 * t + 128] * v for t in range(8)]
    return p + column_sums(acc)


def spread_index():
    return lax.broadcasted_iota(jnp.int32, (8, 128), 1) - lax.broadcasted_iota(jnp.int32, (8, 128), 0)


def halves(x):
    hi = x.astype(BF16)
    return hi, (x - hi.astype(F32)).astype(BF16)


def product(x, hi_ref, lo_ref):
    n = x.shape[0]
    hi, lo = halves(x)
    both = jnp.dot(jnp.concatenate([hi, lo], 0), hi_ref[...], preferred_element_type=F32)
    return both[:n] + both[n:] + jnp.dot(hi, lo_ref[...], preferred_element_type=F32)


def on_rows(words, i, diff):
    q = i // 16
    return wide(jnp.sum(jnp.where(diff == 8 * (i % 16), wide(words[q : q + 1]), 0.0), axis=1, keepdims=True))


def store_bits(bits_ref, words, diff):
    for i in range(64):
        bits_ref[8 * i : 8 * i + 8, :] = on_rows(words, i, diff).astype(jnp.int32)


def store_weighted(hw_ref, h_ref, weight, diff):
    for i in range(64):
        r = slice(8 * i, 8 * i + 8)
        w = on_rows(weight, i, diff)
        for t in range(8):
            c = slice(128 * t, 128 * t + 128)
            hw_ref[r, c] = h_ref[r, c] * w


def prepare(f_ref, h_ref, wait_f, gp_hi, gp_lo, gy_hi, gy_lo, h_hi, h_lo, diag_ref, t_hi, t_lo):
    h_hi[...], h_lo[...] = halves(h_ref[...])
    for j in range(8):
        r = slice(128 * j, 128 * j + 128)
        t_hi[r, :], t_lo[r, :] = halves(jnp.transpose(h_ref[:, r]))
    wait_f()
    for j in range(4):
        r = slice(256 * j, 256 * j + 256)
        ft = jnp.transpose(f_ref[:, r])
        row = lax.broadcasted_iota(jnp.int32, ft.shape, 0) + 256 * j
        on = row == lax.broadcasted_iota(jnp.int32, ft.shape, 1)
        gy_hi[r, :], gy_lo[r, :] = halves(product(ft, t_hi, t_lo))
        gp_hi[r, :], gp_lo[r, :] = halves(jnp.where(on, 0.0, ft))
        diag_ref[:, r] = jnp.sum(jnp.where(on, ft, 0.0), axis=0, keepdims=True)[:, r]


def flat(rows):
    return jnp.concatenate([rows[q : q + 1] for q in range(4)], 1)


def block_kernel(
    at_ref, got_ref, s_ref, weight_ref, f_any, h_any,
    x_own, x_end, maps, map_ends, state, bits_ref, hw_ref, f_ref, h_ref,
    gp_hi, gp_lo, gy_hi, gy_lo, h_hi, h_lo, diag_ref, t_hi, t_lo, sems,
):
    second, own, plane, place = at_ref[0], at_ref[1], at_ref[2], at_ref[3]
    fetch_h = pltpu.make_async_copy(h_any, h_ref, sems.at[0])
    fetch_f = pltpu.make_async_copy(f_any, f_ref, sems.at[1])
    fetch_h.start()
    fetch_f.start()
    fetch_h.wait()

    def at_step(k):
        return got_ref[k % 32, (plane + 4 - k // 32) % 4]


    @pl.when(second == 0)
    def _():
        diff = spread_index()
        maps[...] = jnp.zeros_like(maps)
        map_ends[...] = jnp.zeros_like(map_ends)
        store_weighted(hw_ref, h_ref, weight_ref[...], diff)
        fetch_f.wait()

        def group(g, x):
            words = sum(at_step(16 * g + j)[4:8] * float(2**j) for j in range(16))
            store_bits(bits_ref, words, diff)

            def step(j, x):
                k = 16 * g + j

                @pl.when(k == own)
                def _():
                    x_own[...] = x

                p = propagate(f_ref, x, diff)
                return update(h_ref, hw_ref, bits_ref, jnp.int32(1) << j, at_step(k)[0:4], p, diff)

            return lax.fori_loop(0, 16, step, x)

        x_end[...] = lax.fori_loop(0, 8, group, s_ref[...])

    @pl.when(second != 0)
    def _():
        x_own[...] = jnp.zeros_like(x_own)
        x_end[...] = jnp.zeros_like(x_end)
        prepare(f_ref, h_ref, fetch_f.wait, gp_hi, gp_lo, gy_hi, gy_lo, h_hi, h_lo, diag_ref, t_hi, t_lo)
        unit = (
            lax.broadcasted_iota(jnp.int32, (32, 1024), 1)
            == lax.broadcasted_iota(jnp.int32, (32, 1024), 0) + 32 * place
        ).astype(F32)
        state[0:32, :] = unit
        state[32:64, :] = unit
        state[64:72, :] = jnp.zeros((8, 1024), F32)
        row = lax.broadcasted_iota(jnp.int32, (8, 512), 0)
        weight = flat(weight_ref[...])

        early = plane < 2

        def keep(k):
            k = k - jnp.where(early, 0, 2)

            @pl.when(jnp.logical_and(k >= 0, jnp.logical_and(k // 32 == plane % 2, k % 4 == 0)))
            def _():
                q = (k % 32) // 4
                maps[q, 0:32, :] = jnp.where(early, state[0:32, :], state[32:64, :])
                maps[q, 32:40, :] = jnp.where(early, state[64:72, :], pltpu.roll(state[64:72, :], 7, 0))

        def step(k, carry):
            keep(k)
            x = state[...]
            y = product(x, gy_hi, gy_lo)
            p = product(x, gp_hi, gp_lo) + x * diag_ref[...]
            a, b = at_step(k), at_step(62 + k)
            wa, wb = flat(a[4:8]) * weight, flat(b[4:8]) * weight
            zs = jnp.where(row == 0, flat(a[0:4]), jnp.where(row == 1, flat(b[0:4]), 0.0))
            v = jnp.concatenate(
                [
                    -wa * y[0:32],
                    -wb * y[32:64],
                    jnp.where(row == 0, wa, wb) * (zs - y[64:72]),
                ],
                0,
            )
            state[...] = p + product(v, h_hi, h_lo)
            return carry

        lax.fori_loop(0, 62, step, 0)
        keep(jnp.int32(62))
        map_ends[0:32, :] = state[0:32, :]
        map_ends[32:40, :] = state[64:72, :]


def run_blocks(*args):
    return pl.pallas_call(
        block_kernel,
        out_shape=(
            jax.ShapeDtypeStruct((8, 128), F32),
            jax.ShapeDtypeStruct((8, 128), F32),
            jax.ShapeDtypeStruct((8, 40, 1024), F32),
            jax.ShapeDtypeStruct((40, 1024), F32),
        ),
        in_specs=[SMEM] + [VMEM] * 3 + [ANY] * 2,
        out_specs=(VMEM,) * 4,
        scratch_shapes=[
            pltpu.VMEM((72, 1024), F32),
            pltpu.VMEM((512, 128), jnp.int32),
            pltpu.VMEM((512, 1024), F32),
            pltpu.VMEM((1024, 1024), F32),
            pltpu.VMEM((512, 1024), F32),
            *[pltpu.VMEM((1024, 1024), BF16)] * 2,
            *[pltpu.VMEM((1024, 512), BF16)] * 2,
            *[pltpu.VMEM((512, 1024), BF16)] * 2,
            pltpu.VMEM((1, 1024), F32),
            *[pltpu.VMEM((1024, 512), BF16)] * 2,
            pltpu.SemaphoreType.DMA((2,)),
        ],
        compiler_params=pltpu.CompilerParams(vmem_limit_bytes=58 * 2**20),
        name="blocks",
    )(*args)


def parts_kernel(at_ref, s1_ref, s2_ref, maps_ref, out_ref):
    s2 = jnp.sum(s2_ref[...], axis=0, keepdims=True)
    s = jnp.where(at_ref[2] < 2, s1_ref[...], s2)
    s = jnp.broadcast_to(s, (32, 32))
    on = lax.broadcasted_iota(jnp.int32, (32, 32), 0) == lax.broadcasted_iota(jnp.int32, (32, 32), 1)
    s = jnp.sum(jnp.where(on, s, 0.0), axis=1, keepdims=True)
    once = (at_ref[3] == 0).astype(F32)
    for q in range(8):
        total = jnp.sum(s * maps_ref[q, 0:32, :], axis=0, keepdims=True) + once * maps_ref[q, 32:33, :]
        for j in range(4):
            for t in range(8):
                out_ref[4 * q + j, t : t + 1, :] = total[:, 128 * t : 128 * t + 128]


def run_parts(*args):
    return pl.pallas_call(
        parts_kernel,
        out_shape=jax.ShapeDtypeStruct((32, 8, 128), F32),
        in_specs=[SMEM] + [VMEM] * 3,
        out_specs=VMEM,
        compiler_params=pltpu.CompilerParams(vmem_limit_bytes=6 * 2**20),
        name="parts",
    )(*args)


def own_kernel(
    at_ref, z_ref, m_ref, f_ref, h_ref, weight_ref, d_ref, x_own, got_ref,
    x_out, f_out, e_out, bits_ref, hw_ref, xs, fs,
):
    diff = spread_index()
    store_weighted(hw_ref, h_ref, weight_ref[...], diff)
    store_bits(bits_ref, sum(m_ref[j] * float(2**j) for j in range(4)), diff)

    def step(k, x):
        p = propagate(f_ref, x, diff)

        @pl.when(k > 0)
        def _():
            fs[k - 1] = p

        x = update(h_ref, hw_ref, bits_ref, jnp.int32(1) << k, z_ref[k], p, diff)
        xs[k] = x
        return x

    begin = jnp.where(at_ref[0] == 0, x_own[...], jnp.sum(got_ref[...], axis=0))
    x = lax.fori_loop(0, 4, step, begin)
    fs[3] = propagate(f_ref, x, diff)
    shift = (8 - 2 * at_ref[4]) % 8
    x4 = [pltpu.roll(xs[j], shift, 0)[0:2] for j in range(4)]
    f4 = [pltpu.roll(fs[j], shift, 0)[0:2] for j in range(4)]
    last = at_ref[5] == 63
    factor = jnp.ones((2, 128), F32)
    const = jnp.where(last, f4[3], 0.0)
    for j in reversed(range(4)):
        const = x4[j] + d_ref[j] * (const - f4[j])
        factor = factor * d_ref[j]
        x_out[j] = x4[j]
        f_out[j] = f4[j]
    element = jnp.concatenate([jnp.where(last, 0.0, factor), const], 0)
    e_out[...] = jnp.broadcast_to(element[None], e_out.shape)


def run_own(*args):
    return pl.pallas_call(
        own_kernel,
        out_shape=(
            jax.ShapeDtypeStruct((4, 2, 128), F32),
            jax.ShapeDtypeStruct((4, 2, 128), F32),
            jax.ShapeDtypeStruct((64, 4, 128), F32),
        ),
        in_specs=[SMEM] + [VMEM] * 8,
        out_specs=(VMEM,) * 3,
        scratch_shapes=[
            pltpu.VMEM((512, 128), jnp.int32),
            pltpu.VMEM((512, 1024), F32),
            pltpu.VMEM((4, 8, 128), F32),
            pltpu.VMEM((4, 8, 128), F32),
        ],
        compiler_params=pltpu.CompilerParams(vmem_limit_bytes=12 * 2**20),
        name="own_steps",
    )(*args)


def smooth_kernel(at_ref, parts_ref, d_ref, x_ref, f_ref, x_out, r_out):
    at = at_ref[5]
    later = f_ref[3]
    count = parts_ref.shape[0]

    def one(i, later):
        j = count - 1 - i
        e = parts_ref[j]
        return jnp.where(j > at, e[0:2] * later + e[2:4], later)

    later = lax.fori_loop(0, count, one, later)
    for j in reversed(range(4)):
        x = x_ref[j]
        later = x + d_ref[j] * (later - f_ref[j])
        for q in range(2):
            x_out[j : j + 1, 128 * q : 128 * q + 128] = x[q : q + 1]
            r_out[j : j + 1, 128 * q : 128 * q + 128] = later[q : q + 1]


def run_smooth(*args):
    return pl.pallas_call(
        smooth_kernel,
        out_shape=(jax.ShapeDtypeStruct((4, 256), F32),) * 2,
        in_specs=[SMEM] + [VMEM] * 4,
        out_specs=(VMEM, VMEM),
        compiler_params=pltpu.CompilerParams(vmem_limit_bytes=4 * 2**20),
        name="smooth_own",
    )(*args)


def body(z, mask, f, h, weight, d, prior):
    h_at, l_at = lax.axis_index("h"), lax.axis_index("l")
    at = lax.axis_index(TIME)
    place = lax.axis_index(PLANE)
    y = lax.axis_index("y")
    flags = jnp.stack([h_at, 4 * (at % 32), l_at, place, y, at]).astype(jnp.int32)
    own_z = lax.dynamic_slice_in_dim(z, y, 1, 0).reshape(4, 128)
    own_m = lax.dynamic_slice_in_dim(mask, y, 1, 0).astype(F32).reshape(4, 128)
    own = jnp.concatenate([own_z, own_m], 0)
    turned = [lax.ppermute(own, "l", [(i, (i + n) % 4) for i in range(4)]) for n in (1, 2, 3)]
    own = jnp.broadcast_to(jnp.stack([own, *turned])[None], (32, 4, 8, 128))
    got = lax.all_to_all(own, PLANE, 0, 0, tiled=True)
    weight = weight.reshape(4, 128)
    x_own, x_end, maps, ends = run_blocks(flags, got, prior.reshape(8, 128), weight, f, h)
    s1 = lax.ppermute(x_end, "h", [(0, 1)]).reshape(32, 32)
    s1 = lax.dynamic_slice_in_dim(s1, place, 1, 0)
    part = jnp.sum(s1.reshape(32, 1) * ends[:32], 0) + jnp.where(place == 0, ends[32], 0.0)
    s2 = lax.all_to_all(part.reshape(32, 32), PLANE, 0, 0, tiled=True)
    parts = lax.all_to_all(run_parts(flags, s1, s2, maps), PLANE, 0, 0, tiled=True)
    z4 = z.reshape(4, 4, 128)
    m4 = mask.astype(F32).reshape(4, 4, 128)
    d4 = d.reshape(4, 2, 128)
    x4, f4, element = run_own(flags, z4, m4, f, h, weight, d4, x_own, parts)
    elements = lax.all_to_all(element, TIME, 0, 0, tiled=True)
    return run_smooth(flags, elements, d4, x4, f4)


def solution(mesh):
    fine = Mesh(mesh.devices.reshape(2, 4, 4, 2, 4), TIME + ("y",))
    t = P(TIME, None)
    ty = P(TIME, "y")
    return jax.shard_map(
        body,
        mesh=fine,
        in_specs=(t, t, P(), P(), P(), ty, P()),
        out_specs=(ty, ty),
        check_vma=False,
    )
```

```python
import functools

import jax
import jax.numpy as jnp
from jax import lax
from jax.experimental import pallas as pl
from jax.experimental.pallas import tpu as pltpu
from jax.sharding import Mesh, PartitionSpec as P

F32 = jnp.float32
HALF = ("l", "x", "c", "y")
PLANE = ("x", "c", "y")
TIME = ("h", "l", "x", "c")
BF16 = jnp.bfloat16
VMEM = pl.BlockSpec(memory_space=pltpu.VMEM)
SMEM = pl.BlockSpec(memory_space=pltpu.SMEM)
ANY = pl.BlockSpec(memory_space=pl.ANY)


def wide(row):
    return jnp.broadcast_to(row, (8, 128))


def tree(terms):
    while len(terms) > 1:
        terms = [a + b for a, b in zip(terms[::2], terms[1::2])]
    return terms[0]


def column_sums(blocks):
    return jnp.concatenate([jnp.sum(b, axis=0, keepdims=True) for b in blocks], 0)


def propagate(f_ref, x, diff):
    xs = [wide(x[t : t + 1]) for t in range(8)]
    out = []
    for t in range(8):
        spread = None
        for b in range(16):
            i = 8 * (16 * t + b)
            s = tree([f_ref[i : i + 8, 128 * u : 128 * u + 128] * xs[u] for u in range(8)])
            s = wide(jnp.sum(s, axis=1, keepdims=True))
            spread = jnp.where(diff == 8 * b, s, 0.0 if spread is None else spread)
        out.append(spread)
    return column_sums(out)


def update(h_ref, hw_ref, bits_ref, bit, z, p, diff):
    ps = [wide(p[t : t + 1]) for t in range(8)]
    zs = [wide(z[q : q + 1]) for q in range(4)]
    acc = [jnp.zeros((8, 128), F32) for _ in range(8)]
    for i in range(64):
        r = slice(8 * i, 8 * i + 8)
        s = tree([h_ref[r, 128 * t : 128 * t + 128] * ps[t] for t in range(8)])
        s = jnp.where(diff == 8 * (i % 16), zs[i // 16], 0.0) - s
        s = wide(jnp.sum(s, axis=1, keepdims=True))
        v = jnp.where((bits_ref[r, :] & bit) != 0, s, 0.0)
        acc = [acc[t] + hw_ref[r, 128 * t : 128 * t + 128] * v for t in range(8)]
    return p + column_sums(acc)


def spread_index():
    return lax.broadcasted_iota(jnp.int32, (8, 128), 1) - lax.broadcasted_iota(jnp.int32, (8, 128), 0)


def halves(x):
    hi = x.astype(BF16)
    return hi, (x - hi.astype(F32)).astype(BF16)


def product(x, hi_ref, lo_ref):
    n = x.shape[0]
    hi, lo = halves(x)
    both = jnp.dot(jnp.concatenate([hi, lo], 0), hi_ref[...], preferred_element_type=F32)
    return both[:n] + both[n:] + jnp.dot(hi, lo_ref[...], preferred_element_type=F32)


def on_rows(words, i, diff):
    q = i // 16
    return wide(jnp.sum(jnp.where(diff == 8 * (i % 16), wide(words[q : q + 1]), 0.0), axis=1, keepdims=True))


def store_bits(bits_ref, words, diff):
    for i in range(64):
        bits_ref[8 * i : 8 * i + 8, :] = on_rows(words, i, diff).astype(jnp.int32)


def store_weighted(hw_ref, h_ref, weight, diff):
    for i in range(64):
        r = slice(8 * i, 8 * i + 8)
        w = on_rows(weight, i, diff)
        for t in range(8):
            c = slice(128 * t, 128 * t + 128)
            hw_ref[r, c] = h_ref[r, c] * w


def prepare_kernel(
    f_any, h_any, gy_hi, gy_lo, gx_hi, gx_lo, diag_ref,
    f_ref, h_ref, y_hi, y_lo, x_hi, x_lo, t_hi, t_lo, in_sems, out_sems,
):
    fetch_h = pltpu.make_async_copy(h_any, h_ref, in_sems.at[0])
    fetch_f = pltpu.make_async_copy(f_any, f_ref, in_sems.at[1])
    fetch_h.start()
    fetch_f.start()
    fetch_h.wait()
    sent = []

    def send(source, target, r):
        copy = pltpu.make_async_copy(source.at[r], target.at[r], out_sems.at[len(sent)])
        copy.start()
        sent.append(copy)

    low = pl.ds(1024, 512)
    x_hi[low, :], x_lo[low, :] = halves(h_ref[...])
    send(x_hi, gx_hi, low)
    send(x_lo, gx_lo, low)
    for j in range(8):
        r = slice(128 * j, 128 * j + 128)
        t_hi[r, :], t_lo[r, :] = halves(jnp.transpose(h_ref[:, r]))
    fetch_f.wait()
    for j in range(4):
        r = slice(256 * j, 256 * j + 256)
        ft = jnp.transpose(f_ref[:, r])
        row = lax.broadcasted_iota(jnp.int32, ft.shape, 0) + 256 * j
        on = row == lax.broadcasted_iota(jnp.int32, ft.shape, 1)
        x_hi[r, :], x_lo[r, :] = halves(jnp.where(on, 0.0, ft))
        diag_ref[:, r] = jnp.sum(jnp.where(on, ft, 0.0), axis=0, keepdims=True)[:, r]
        block = pl.ds(256 * j, 256)
        send(x_hi, gx_hi, block)
        send(x_lo, gx_lo, block)
        y_hi[r, :], y_lo[r, :] = halves(product(ft, t_hi, t_lo))
        send(y_hi, gy_hi, block)
        send(y_lo, gy_lo, block)
    for copy in sent:
        copy.wait()


def prepare(f, h):
    outs = [((1024, 512), BF16)] * 2 + [((1536, 1024), BF16)] * 2
    return pl.pallas_call(
        prepare_kernel,
        out_shape=(*[jax.ShapeDtypeStruct(*o) for o in outs], jax.ShapeDtypeStruct((1, 1024), F32)),
        in_specs=[ANY] * 2,
        out_specs=(*[ANY] * 4, VMEM),
        scratch_shapes=[
            pltpu.VMEM((1024, 1024), F32),
            pltpu.VMEM((512, 1024), F32),
            *[pltpu.VMEM(*o) for o in outs],
            *[pltpu.VMEM((1024, 512), BF16)] * 2,
            pltpu.SemaphoreType.DMA((2,)),
            pltpu.SemaphoreType.DMA((18,)),
        ],
        compiler_params=pltpu.CompilerParams(vmem_limit_bytes=58 * 2**20),
        cost_estimate=pl.CostEstimate(flops=3 * 2**30, bytes_accessed=14 * 2**20, transcendentals=0),
        name="prepare",
    )(f, h)


def flat(rows):
    return jnp.concatenate([rows[q : q + 1] for q in range(4)], 1)


def block_kernel(
    at_ref, got_ref, s_ref, weight_ref, diag_ref, f_any, h_any, *rest,
):
    mats_any, (x_own, x_end, maps, map_ends), rest = rest[:4], rest[4:8], rest[8:]
    state, bits_ref, hw_ref, f_ref, h_ref, *mats, sems = rest
    gy_hi, gy_lo, gx_hi, gx_lo = mats
    second, own, plane, place = at_ref[0], at_ref[1], at_ref[2], at_ref[3]

    def fetch(pairs):
        copies = [pltpu.make_async_copy(a, b, sems.at[i]) for i, (a, b) in enumerate(pairs)]
        for c in copies:
            c.start()
        for c in copies:
            c.wait()

    def at_step(k):
        return got_ref[k % 32, (plane + 4 - k // 32) % 4]


    @pl.when(second == 0)
    def _():
        fetch([(f_any, f_ref), (h_any, h_ref)])
        diff = spread_index()
        maps[...] = jnp.zeros_like(maps)
        map_ends[...] = jnp.zeros_like(map_ends)
        store_weighted(hw_ref, h_ref, weight_ref[...], diff)

        def group(g, x):
            words = sum(at_step(16 * g + j)[4:8] * float(2**j) for j in range(16))
            store_bits(bits_ref, words, diff)

            def step(j, x):
                k = 16 * g + j

                @pl.when(k == own)
                def _():
                    x_own[...] = x

                p = propagate(f_ref, x, diff)
                return update(h_ref, hw_ref, bits_ref, jnp.int32(1) << j, at_step(k)[0:4], p, diff)

            return lax.fori_loop(0, 16, step, x)

        x_end[...] = lax.fori_loop(0, 8, group, s_ref[...])

    @pl.when(second != 0)
    def _():
        x_own[...] = jnp.zeros_like(x_own)
        x_end[...] = jnp.zeros_like(x_end)
        fetch(list(zip(mats_any, mats)))
        unit = (
            lax.broadcasted_iota(jnp.int32, (32, 1024), 1)
            == lax.broadcasted_iota(jnp.int32, (32, 1024), 0) + 32 * place
        ).astype(F32)
        state[0:32, :] = unit
        state[32:64, :] = unit
        state[64:72, :] = jnp.zeros((8, 1024), F32)
        row = lax.broadcasted_iota(jnp.int32, (8, 512), 0)
        weight = flat(weight_ref[...])

        early = plane < 2

        def keep(k):
            k = k - jnp.where(early, 0, 2)

            @pl.when(jnp.logical_and(k >= 0, jnp.logical_and(k // 32 == plane % 2, k % 4 == 0)))
            def _():
                q = (k % 32) // 4
                maps[q, 0:32, :] = jnp.where(early, state[0:32, :], state[32:64, :])
                maps[q, 32:40, :] = jnp.where(early, state[64:72, :], pltpu.roll(state[64:72, :], 7, 0))

        def step(k, carry):
            keep(k)
            x = state[...]
            hi, lo = halves(x)
            both = jnp.concatenate([hi, lo], 0)
            y = jnp.dot(both, gy_hi[...], preferred_element_type=F32)
            y = y[:72] + y[72:] + jnp.dot(hi, gy_lo[...], preferred_element_type=F32)
            a, b = at_step(k), at_step(62 + k)
            wa, wb = flat(a[4:8]) * weight, flat(b[4:8]) * weight
            zs = jnp.where(row == 0, flat(a[0:4]), jnp.where(row == 1, flat(b[0:4]), 0.0))
            v = jnp.concatenate(
                [
                    -wa * y[0:32],
                    -wb * y[32:64],
                    jnp.where(row == 0, wa, wb) * (zs - y[64:72]),
                ],
                0,
            )
            v_hi, v_lo = halves(v)
            both = jnp.concatenate([both, jnp.concatenate([v_hi, v_lo], 0)], 1)
            hi = jnp.concatenate([hi, v_hi], 1)
            for j in range(4):
                r = slice(256 * j, 256 * j + 256)
                out = jnp.dot(both, gx_hi[:, r], preferred_element_type=F32)
                out = out[:72] + out[72:] + jnp.dot(hi, gx_lo[:, r], preferred_element_type=F32)
                state[:, r] = out + x[:, r] * diag_ref[:, r]
            return carry

        lax.fori_loop(0, 62, step, 0)
        keep(jnp.int32(62))
        map_ends[0:32, :] = state[0:32, :]
        map_ends[32:40, :] = state[64:72, :]


def run_blocks(*args):
    return pl.pallas_call(
        block_kernel,
        out_shape=(
            jax.ShapeDtypeStruct((8, 128), F32),
            jax.ShapeDtypeStruct((8, 128), F32),
            jax.ShapeDtypeStruct((8, 40, 1024), F32),
            jax.ShapeDtypeStruct((40, 1024), F32),
        ),
        in_specs=[SMEM] + [VMEM] * 4 + [ANY] * 6,
        out_specs=(VMEM,) * 4,
        scratch_shapes=[
            pltpu.VMEM((72, 1024), F32),
            pltpu.VMEM((512, 128), jnp.int32),
            pltpu.VMEM((512, 1024), F32),
            pltpu.VMEM((1024, 1024), F32),
            pltpu.VMEM((512, 1024), F32),
            *[pltpu.VMEM((1024, 512), BF16)] * 2,
            *[pltpu.VMEM((1536, 1024), BF16)] * 2,
            pltpu.SemaphoreType.DMA((4,)),
        ],
        compiler_params=pltpu.CompilerParams(vmem_limit_bytes=58 * 2**20),
        name="blocks",
    )(*args)


def parts_kernel(at_ref, s1_ref, s2_ref, maps_ref, out_ref):
    s2 = jnp.sum(s2_ref[...], axis=0, keepdims=True)
    s = jnp.where(at_ref[2] < 2, s1_ref[...], s2)
    s = jnp.broadcast_to(s, (32, 32))
    on = lax.broadcasted_iota(jnp.int32, (32, 32), 0) == lax.broadcasted_iota(jnp.int32, (32, 32), 1)
    s = jnp.sum(jnp.where(on, s, 0.0), axis=1, keepdims=True)
    once = (at_ref[3] == 0).astype(F32)
    for q in range(8):
        total = jnp.sum(s * maps_ref[q, 0:32, :], axis=0, keepdims=True) + once * maps_ref[q, 32:33, :]
        for j in range(4):
            for t in range(8):
                out_ref[4 * q + j, t : t + 1, :] = total[:, 128 * t : 128 * t + 128]


def run_parts(*args):
    return pl.pallas_call(
        parts_kernel,
        out_shape=jax.ShapeDtypeStruct((32, 8, 128), F32),
        in_specs=[SMEM] + [VMEM] * 3,
        out_specs=VMEM,
        compiler_params=pltpu.CompilerParams(vmem_limit_bytes=6 * 2**20),
        name="parts",
    )(*args)


def own_kernel(
    at_ref, z_ref, m_ref, f_ref, h_ref, weight_ref, d_ref, x_own, got_ref,
    x_out, f_out, e_out, bits_ref, hw_ref, xs, fs,
):
    diff = spread_index()
    store_weighted(hw_ref, h_ref, weight_ref[...], diff)
    store_bits(bits_ref, sum(m_ref[j] * float(2**j) for j in range(4)), diff)

    def step(k, x):
        p = propagate(f_ref, x, diff)

        @pl.when(k > 0)
        def _():
            fs[k - 1] = p

        x = update(h_ref, hw_ref, bits_ref, jnp.int32(1) << k, z_ref[k], p, diff)
        xs[k] = x
        return x

    begin = jnp.where(at_ref[0] == 0, x_own[...], jnp.sum(got_ref[...], axis=0))
    x = lax.fori_loop(0, 4, step, begin)
    fs[3] = propagate(f_ref, x, diff)
    shift = (8 - 2 * at_ref[4]) % 8
    x4 = [pltpu.roll(xs[j], shift, 0)[0:2] for j in range(4)]
    f4 = [pltpu.roll(fs[j], shift, 0)[0:2] for j in range(4)]
    last = at_ref[5] == 63
    factor = jnp.ones((2, 128), F32)
    const = jnp.where(last, f4[3], 0.0)
    for j in reversed(range(4)):
        const = x4[j] + d_ref[j] * (const - f4[j])
        factor = factor * d_ref[j]
        x_out[j] = x4[j]
        f_out[j] = f4[j]
    element = jnp.concatenate([jnp.where(last, 0.0, factor), const], 0)
    e_out[...] = jnp.broadcast_to(element[None], e_out.shape)


def run_own(*args):
    return pl.pallas_call(
        own_kernel,
        out_shape=(
            jax.ShapeDtypeStruct((4, 2, 128), F32),
            jax.ShapeDtypeStruct((4, 2, 128), F32),
            jax.ShapeDtypeStruct((64, 4, 128), F32),
        ),
        in_specs=[SMEM] + [VMEM] * 8,
        out_specs=(VMEM,) * 3,
        scratch_shapes=[
            pltpu.VMEM((512, 128), jnp.int32),
            pltpu.VMEM((512, 1024), F32),
            pltpu.VMEM((4, 8, 128), F32),
            pltpu.VMEM((4, 8, 128), F32),
        ],
        compiler_params=pltpu.CompilerParams(vmem_limit_bytes=12 * 2**20),
        name="own_steps",
    )(*args)


def smooth_kernel(at_ref, parts_ref, d_ref, x_ref, f_ref, x_out, r_out):
    at = at_ref[5]
    later = f_ref[3]
    count = parts_ref.shape[0]

    def one(i, later):
        j = count - 1 - i
        e = parts_ref[j]
        return jnp.where(j > at, e[0:2] * later + e[2:4], later)

    later = lax.fori_loop(0, count, one, later)
    for j in reversed(range(4)):
        x = x_ref[j]
        later = x + d_ref[j] * (later - f_ref[j])
        for q in range(2):
            x_out[j : j + 1, 128 * q : 128 * q + 128] = x[q : q + 1]
            r_out[j : j + 1, 128 * q : 128 * q + 128] = later[q : q + 1]


def run_smooth(*args):
    return pl.pallas_call(
        smooth_kernel,
        out_shape=(jax.ShapeDtypeStruct((4, 256), F32),) * 2,
        in_specs=[SMEM] + [VMEM] * 4,
        out_specs=(VMEM, VMEM),
        compiler_params=pltpu.CompilerParams(vmem_limit_bytes=4 * 2**20),
        name="smooth_own",
    )(*args)


def body(z, mask, f, h, weight, d, prior):
    h_at, l_at = lax.axis_index("h"), lax.axis_index("l")
    at = lax.axis_index(TIME)
    place = lax.axis_index(PLANE)
    y = lax.axis_index("y")
    flags = jnp.stack([h_at, 4 * (at % 32), l_at, place, y, at]).astype(jnp.int32)
    own_z = lax.dynamic_slice_in_dim(z, y, 1, 0).reshape(4, 128)
    own_m = lax.dynamic_slice_in_dim(mask, y, 1, 0).astype(F32).reshape(4, 128)
    own = jnp.concatenate([own_z, own_m], 0)
    turned = [lax.ppermute(own, "l", [(i, (i + n) % 4) for i in range(4)]) for n in (1, 2, 3)]
    *mats, diag = prepare(f, h)
    own = jnp.broadcast_to(jnp.stack([own, *turned])[None], (32, 4, 8, 128))
    got = lax.all_to_all(own, PLANE, 0, 0, tiled=True)
    weight = weight.reshape(4, 128)
    x_own, x_end, maps, ends = run_blocks(flags, got, prior.reshape(8, 128), weight, diag, f, h, *mats)
    s1 = lax.ppermute(x_end, "h", [(0, 1)]).reshape(32, 32)
    s1 = lax.dynamic_slice_in_dim(s1, place, 1, 0)
    part = jnp.sum(s1.reshape(32, 1) * ends[:32], 0) + jnp.where(place == 0, ends[32], 0.0)
    s2 = lax.all_to_all(part.reshape(32, 32), PLANE, 0, 0, tiled=True)
    parts = lax.all_to_all(run_parts(flags, s1, s2, maps), PLANE, 0, 0, tiled=True)
    z4 = z.reshape(4, 4, 128)
    m4 = mask.astype(F32).reshape(4, 4, 128)
    d4 = d.reshape(4, 2, 128)
    x4, f4, element = run_own(flags, z4, m4, f, h, weight, d4, x_own, parts)
    elements = lax.all_to_all(element, TIME, 0, 0, tiled=True)
    return run_smooth(flags, elements, d4, x4, f4)


def solution(mesh):
    fine = Mesh(mesh.devices.reshape(2, 4, 4, 2, 4), TIME + ("y",))
    t = P(TIME, None)
    ty = P(TIME, "y")
    return jax.shard_map(
        body,
        mesh=fine,
        in_specs=(t, t, P(), P(), P(), ty, P()),
        out_specs=(ty, ty),
        check_vma=False,
    )
```

```python
import functools

import jax
import jax.numpy as jnp
from jax import lax
from jax.experimental import pallas as pl
from jax.experimental.pallas import tpu as pltpu
from jax.sharding import Mesh, PartitionSpec as P

F32 = jnp.float32
HALF = ("l", "x", "c", "y")
PLANE = ("x", "c", "y")
TIME = ("h", "l", "x", "c")
BF16 = jnp.bfloat16
VMEM = pl.BlockSpec(memory_space=pltpu.VMEM)
SMEM = pl.BlockSpec(memory_space=pltpu.SMEM)
ANY = pl.BlockSpec(memory_space=pl.ANY)


def wide(row):
    return jnp.broadcast_to(row, (8, 128))


def tree(terms):
    while len(terms) > 1:
        terms = [a + b for a, b in zip(terms[::2], terms[1::2])]
    return terms[0]


def column_sums(blocks):
    return jnp.concatenate([jnp.sum(b, axis=0, keepdims=True) for b in blocks], 0)


def propagate(f_ref, x, diff):
    xs = [wide(x[t : t + 1]) for t in range(8)]
    out = []
    for t in range(8):
        spread = None
        for b in range(16):
            i = 8 * (16 * t + b)
            s = tree([f_ref[i : i + 8, 128 * u : 128 * u + 128] * xs[u] for u in range(8)])
            s = wide(jnp.sum(s, axis=1, keepdims=True))
            spread = jnp.where(diff == 8 * b, s, 0.0 if spread is None else spread)
        out.append(spread)
    return column_sums(out)


def update(h_ref, hw_ref, bits_ref, bit, z, p, diff):
    ps = [wide(p[t : t + 1]) for t in range(8)]
    zs = [wide(z[q : q + 1]) for q in range(4)]
    acc = [jnp.zeros((8, 128), F32) for _ in range(8)]
    for i in range(64):
        r = slice(8 * i, 8 * i + 8)
        s = tree([h_ref[r, 128 * t : 128 * t + 128] * ps[t] for t in range(8)])
        s = jnp.where(diff == 8 * (i % 16), zs[i // 16], 0.0) - s
        s = wide(jnp.sum(s, axis=1, keepdims=True))
        v = jnp.where((bits_ref[r, :] & bit) != 0, s, 0.0)
        acc = [acc[t] + hw_ref[r, 128 * t : 128 * t + 128] * v for t in range(8)]
    return p + column_sums(acc)


def spread_index():
    return lax.broadcasted_iota(jnp.int32, (8, 128), 1) - lax.broadcasted_iota(jnp.int32, (8, 128), 0)


def halves(x):
    hi = x.astype(BF16)
    return hi, (x - hi.astype(F32)).astype(BF16)


def product(x, hi_ref, lo_ref):
    n = x.shape[0]
    hi, lo = halves(x)
    both = jnp.dot(jnp.concatenate([hi, lo], 0), hi_ref[...], preferred_element_type=F32)
    return both[:n] + both[n:] + jnp.dot(hi, lo_ref[...], preferred_element_type=F32)


def on_rows(words, i, diff):
    q = i // 16
    return wide(jnp.sum(jnp.where(diff == 8 * (i % 16), wide(words[q : q + 1]), 0.0), axis=1, keepdims=True))


def store_bits(bits_ref, words, diff):
    for i in range(64):
        bits_ref[8 * i : 8 * i + 8, :] = on_rows(words, i, diff).astype(jnp.int32)


def store_weighted(hw_ref, h_ref, weight, diff):
    for i in range(64):
        r = slice(8 * i, 8 * i + 8)
        w = on_rows(weight, i, diff)
        for t in range(8):
            c = slice(128 * t, 128 * t + 128)
            hw_ref[r, c] = h_ref[r, c] * w


def prepare_kernel(
    f_any, h_any, gy_hi, gy_lo, gx_hi, gx_lo, diag_ref,
    f_ref, h_ref, y_hi, y_lo, x_hi, x_lo, t_hi, t_lo, in_sems, out_sems,
):
    fetch_h = pltpu.make_async_copy(h_any, h_ref, in_sems.at[0])
    fetch_f = pltpu.make_async_copy(f_any, f_ref, in_sems.at[1])
    fetch_h.start()
    fetch_f.start()
    fetch_h.wait()
    sent = []

    def send(source, target, r):
        copy = pltpu.make_async_copy(source.at[r], target.at[r], out_sems.at[len(sent)])
        copy.start()
        sent.append(copy)

    low = pl.ds(1024, 512)
    x_hi[low, :], x_lo[low, :] = halves(h_ref[...])
    send(x_hi, gx_hi, low)
    send(x_lo, gx_lo, low)
    for j in range(8):
        r = slice(128 * j, 128 * j + 128)
        t_hi[r, :], t_lo[r, :] = halves(jnp.transpose(h_ref[:, r]))
    fetch_f.wait()
    for j in range(4):
        r = slice(256 * j, 256 * j + 256)
        ft = jnp.transpose(f_ref[:, r])
        row = lax.broadcasted_iota(jnp.int32, ft.shape, 0) + 256 * j
        on = row == lax.broadcasted_iota(jnp.int32, ft.shape, 1)
        x_hi[r, :], x_lo[r, :] = halves(jnp.where(on, 0.0, ft))
        diag_ref[:, r] = jnp.sum(jnp.where(on, ft, 0.0), axis=0, keepdims=True)[:, r]
        block = pl.ds(256 * j, 256)
        send(x_hi, gx_hi, block)
        send(x_lo, gx_lo, block)
        y_hi[r, :], y_lo[r, :] = halves(product(ft, t_hi, t_lo))
        send(y_hi, gy_hi, block)
        send(y_lo, gy_lo, block)
    for copy in sent:
        copy.wait()


def prepare(f, h):
    outs = [((1024, 512), BF16)] * 2 + [((1536, 1024), BF16)] * 2
    return pl.pallas_call(
        prepare_kernel,
        out_shape=(*[jax.ShapeDtypeStruct(*o) for o in outs], jax.ShapeDtypeStruct((1, 1024), F32)),
        in_specs=[ANY] * 2,
        out_specs=(*[ANY] * 4, VMEM),
        scratch_shapes=[
            pltpu.VMEM((1024, 1024), F32),
            pltpu.VMEM((512, 1024), F32),
            *[pltpu.VMEM(*o) for o in outs],
            *[pltpu.VMEM((1024, 512), BF16)] * 2,
            pltpu.SemaphoreType.DMA((2,)),
            pltpu.SemaphoreType.DMA((18,)),
        ],
        compiler_params=pltpu.CompilerParams(vmem_limit_bytes=58 * 2**20),
        cost_estimate=pl.CostEstimate(flops=3 * 2**30, bytes_accessed=14 * 2**20, transcendentals=0),
        name="prepare",
    )(f, h)


def flat(rows):
    return jnp.concatenate([rows[q : q + 1] for q in range(4)], 1)


def block_kernel(
    at_ref, got_ref, s_ref, weight_ref, diag_ref, f_any, h_any, *rest,
):
    mats_any, (x_own, x_end, maps, map_ends), rest = rest[:4], rest[4:8], rest[8:]
    state, bits_ref, hw_ref, f_ref, h_ref, *mats, sems = rest
    gy_hi, gy_lo, gx_hi, gx_lo = mats
    second, own, plane, place = at_ref[0], at_ref[1], at_ref[2], at_ref[3]

    def fetch(pairs):
        copies = [pltpu.make_async_copy(a, b, sems.at[i]) for i, (a, b) in enumerate(pairs)]
        for c in copies:
            c.start()
        for c in copies:
            c.wait()

    def at_step(k):
        return got_ref[k % 32, (plane + 4 - k // 32) % 4]


    @pl.when(second == 0)
    def _():
        fetch([(f_any, f_ref), (h_any, h_ref)])
        diff = spread_index()
        maps[...] = jnp.zeros_like(maps)
        map_ends[...] = jnp.zeros_like(map_ends)
        store_weighted(hw_ref, h_ref, weight_ref[...], diff)

        def group(g, x):
            words = sum(at_step(16 * g + j)[4:8] * float(2**j) for j in range(16))
            store_bits(bits_ref, words, diff)

            def step(j, x):
                k = 16 * g + j

                @pl.when(k == own)
                def _():
                    x_own[...] = x

                p = propagate(f_ref, x, diff)
                return update(h_ref, hw_ref, bits_ref, jnp.int32(1) << j, at_step(k)[0:4], p, diff)

            return lax.fori_loop(0, 16, step, x)

        x_end[...] = lax.fori_loop(0, 8, group, s_ref[...])

    @pl.when(second != 0)
    def _():
        x_own[...] = jnp.zeros_like(x_own)
        x_end[...] = jnp.zeros_like(x_end)
        fetch(list(zip(mats_any, mats)))
        unit = (
            lax.broadcasted_iota(jnp.int32, (32, 1024), 1)
            == lax.broadcasted_iota(jnp.int32, (32, 1024), 0) + 32 * place
        ).astype(F32)
        state[0:32, :] = unit
        state[32:64, :] = unit
        state[64:72, :] = jnp.zeros((8, 1024), F32)
        row = lax.broadcasted_iota(jnp.int32, (8, 512), 0)
        weight = flat(weight_ref[...])

        early = plane < 2

        def keep(k):
            k = k - jnp.where(early, 0, 2)

            @pl.when(jnp.logical_and(k >= 0, jnp.logical_and(k // 32 == plane % 2, k % 4 == 0)))
            def _():
                q = (k % 32) // 4
                maps[q, 0:32, :] = jnp.where(early, state[0:32, :], state[32:64, :])
                maps[q, 32:40, :] = jnp.where(early, state[64:72, :], pltpu.roll(state[64:72, :], 7, 0))

        def step(k, carry):
            keep(k)
            x = state[...]
            hi, lo = halves(x)
            both = jnp.concatenate([hi, lo], 0)
            y = jnp.dot(both, gy_hi[...], preferred_element_type=F32)
            y = y[:72] + y[72:] + jnp.dot(hi, gy_lo[...], preferred_element_type=F32)
            a, b = at_step(k), at_step(62 + k)
            wa, wb = flat(a[4:8]) * weight, flat(b[4:8]) * weight
            zs = jnp.where(row == 0, flat(a[0:4]), jnp.where(row == 1, flat(b[0:4]), 0.0))
            v = jnp.concatenate(
                [
                    -wa * y[0:32],
                    -wb * y[32:64],
                    jnp.where(row == 0, wa, wb) * (zs - y[64:72]),
                ],
                0,
            )
            v_hi, v_lo = halves(v)
            both = jnp.concatenate([both, jnp.concatenate([v_hi, v_lo], 0)], 1)
            hi = jnp.concatenate([hi, v_hi], 1)
            for j in range(4):
                r = slice(256 * j, 256 * j + 256)
                out = jnp.dot(both, gx_hi[:, r], preferred_element_type=F32)
                out = out[:72] + out[72:] + jnp.dot(hi, gx_lo[:, r], preferred_element_type=F32)
                state[:, r] = out + x[:, r] * diag_ref[:, r]
            return carry

        lax.fori_loop(0, 62, step, 0)
        keep(jnp.int32(62))
        map_ends[0:32, :] = state[0:32, :]
        map_ends[32:40, :] = state[64:72, :]


def run_blocks(*args):
    return pl.pallas_call(
        block_kernel,
        out_shape=(
            jax.ShapeDtypeStruct((8, 128), F32),
            jax.ShapeDtypeStruct((8, 128), F32),
            jax.ShapeDtypeStruct((8, 40, 1024), F32),
            jax.ShapeDtypeStruct((40, 1024), F32),
        ),
        in_specs=[SMEM] + [VMEM] * 4 + [ANY] * 6,
        out_specs=(VMEM,) * 4,
        scratch_shapes=[
            pltpu.VMEM((72, 1024), F32),
            pltpu.VMEM((512, 128), jnp.int32),
            pltpu.VMEM((512, 1024), F32),
            pltpu.VMEM((1024, 1024), F32),
            pltpu.VMEM((512, 1024), F32),
            *[pltpu.VMEM((1024, 512), BF16)] * 2,
            *[pltpu.VMEM((1536, 1024), BF16)] * 2,
            pltpu.SemaphoreType.DMA((4,)),
        ],
        compiler_params=pltpu.CompilerParams(vmem_limit_bytes=58 * 2**20),
        name="blocks",
    )(*args)


def parts_kernel(at_ref, s1_ref, s2_ref, maps_ref, out_ref):
    s2 = jnp.sum(s2_ref[...], axis=0, keepdims=True)
    s = jnp.where(at_ref[2] < 2, s1_ref[...], s2)
    s = jnp.broadcast_to(s, (32, 32))
    on = lax.broadcasted_iota(jnp.int32, (32, 32), 0) == lax.broadcasted_iota(jnp.int32, (32, 32), 1)
    s = jnp.sum(jnp.where(on, s, 0.0), axis=1, keepdims=True)
    once = (at_ref[3] == 0).astype(F32)
    for q in range(8):
        total = jnp.sum(s * maps_ref[q, 0:32, :], axis=0, keepdims=True) + once * maps_ref[q, 32:33, :]
        for j in range(4):
            for t in range(8):
                out_ref[4 * q + j, t : t + 1, :] = total[:, 128 * t : 128 * t + 128]


def run_parts(*args):
    return pl.pallas_call(
        parts_kernel,
        out_shape=jax.ShapeDtypeStruct((32, 8, 128), F32),
        in_specs=[SMEM] + [VMEM] * 3,
        out_specs=VMEM,
        compiler_params=pltpu.CompilerParams(vmem_limit_bytes=6 * 2**20),
        name="parts",
    )(*args)


def own_kernel(
    at_ref, z_ref, m_ref, f_any, h_any, weight_ref, d_ref, x_own, got_ref,
    x_out, f_out, e_out, bits_ref, hw_ref, xs, fs, f_ref, h_ref, sems,
):
    fetch_h = pltpu.make_async_copy(h_any, h_ref, sems.at[0])
    fetch_f = pltpu.make_async_copy(f_any, f_ref, sems.at[1])
    fetch_h.start()
    fetch_f.start()
    diff = spread_index()
    store_bits(bits_ref, sum(m_ref[j] * float(2**j) for j in range(4)), diff)
    fetch_h.wait()
    store_weighted(hw_ref, h_ref, weight_ref[...], diff)
    fetch_f.wait()

    def step(k, x):
        p = propagate(f_ref, x, diff)

        @pl.when(k > 0)
        def _():
            fs[k - 1] = p

        x = update(h_ref, hw_ref, bits_ref, jnp.int32(1) << k, z_ref[k], p, diff)
        xs[k] = x
        return x

    begin = jnp.where(at_ref[0] == 0, x_own[...], jnp.sum(got_ref[...], axis=0))
    x = lax.fori_loop(0, 4, step, begin)
    fs[3] = propagate(f_ref, x, diff)
    shift = (8 - 2 * at_ref[4]) % 8
    x4 = [pltpu.roll(xs[j], shift, 0)[0:2] for j in range(4)]
    f4 = [pltpu.roll(fs[j], shift, 0)[0:2] for j in range(4)]
    last = at_ref[5] == 63
    factor = jnp.ones((2, 128), F32)
    const = jnp.where(last, f4[3], 0.0)
    for j in reversed(range(4)):
        const = x4[j] + d_ref[j] * (const - f4[j])
        factor = factor * d_ref[j]
        x_out[j] = x4[j]
        f_out[j] = f4[j]
    element = jnp.concatenate([jnp.where(last, 0.0, factor), const], 0)
    e_out[...] = jnp.broadcast_to(element[None], e_out.shape)


def run_own(*args):
    return pl.pallas_call(
        own_kernel,
        out_shape=(
            jax.ShapeDtypeStruct((4, 2, 128), F32),
            jax.ShapeDtypeStruct((4, 2, 128), F32),
            jax.ShapeDtypeStruct((64, 4, 128), F32),
        ),
        in_specs=[SMEM] + [VMEM] * 2 + [ANY] * 2 + [VMEM] * 4,
        out_specs=(VMEM,) * 3,
        scratch_shapes=[
            pltpu.VMEM((512, 128), jnp.int32),
            pltpu.VMEM((512, 1024), F32),
            pltpu.VMEM((4, 8, 128), F32),
            pltpu.VMEM((4, 8, 128), F32),
            pltpu.VMEM((1024, 1024), F32),
            pltpu.VMEM((512, 1024), F32),
            pltpu.SemaphoreType.DMA((2,)),
        ],
        compiler_params=pltpu.CompilerParams(vmem_limit_bytes=58 * 2**20),
        name="own_steps",
    )(*args)


def smooth_kernel(at_ref, parts_ref, d_ref, x_ref, f_ref, x_out, r_out):
    at = at_ref[5]
    later = f_ref[3]
    count = parts_ref.shape[0]

    def one(i, later):
        j = count - 1 - i
        e = parts_ref[j]
        return jnp.where(j > at, e[0:2] * later + e[2:4], later)

    later = lax.fori_loop(0, count, one, later)
    for j in reversed(range(4)):
        x = x_ref[j]
        later = x + d_ref[j] * (later - f_ref[j])
        for q in range(2):
            x_out[j : j + 1, 128 * q : 128 * q + 128] = x[q : q + 1]
            r_out[j : j + 1, 128 * q : 128 * q + 128] = later[q : q + 1]


def run_smooth(*args):
    return pl.pallas_call(
        smooth_kernel,
        out_shape=(jax.ShapeDtypeStruct((4, 256), F32),) * 2,
        in_specs=[SMEM] + [VMEM] * 4,
        out_specs=(VMEM, VMEM),
        compiler_params=pltpu.CompilerParams(vmem_limit_bytes=4 * 2**20),
        name="smooth_own",
    )(*args)


def body(z, mask, f, h, weight, d, prior):
    h_at, l_at = lax.axis_index("h"), lax.axis_index("l")
    at = lax.axis_index(TIME)
    place = lax.axis_index(PLANE)
    y = lax.axis_index("y")
    flags = jnp.stack([h_at, 4 * (at % 32), l_at, place, y, at]).astype(jnp.int32)
    own_z = lax.dynamic_slice_in_dim(z, y, 1, 0).reshape(4, 128)
    own_m = lax.dynamic_slice_in_dim(mask, y, 1, 0).astype(F32).reshape(4, 128)
    own = jnp.concatenate([own_z, own_m], 0)
    turned = [lax.ppermute(own, "l", [(i, (i + n) % 4) for i in range(4)]) for n in (1, 2, 3)]
    *mats, diag = prepare(f, h)
    own = jnp.broadcast_to(jnp.stack([own, *turned])[None], (32, 4, 8, 128))
    got = lax.all_to_all(own, PLANE, 0, 0, tiled=True)
    weight = weight.reshape(4, 128)
    x_own, x_end, maps, ends = run_blocks(flags, got, prior.reshape(8, 128), weight, diag, f, h, *mats)
    s1 = lax.ppermute(x_end, "h", [(0, 1)]).reshape(32, 32)
    s1 = lax.dynamic_slice_in_dim(s1, place, 1, 0)
    part = jnp.sum(s1.reshape(32, 1) * ends[:32], 0) + jnp.where(place == 0, ends[32], 0.0)
    s2 = lax.all_to_all(part.reshape(32, 32), PLANE, 0, 0, tiled=True)
    parts = lax.all_to_all(run_parts(flags, s1, s2, maps), PLANE, 0, 0, tiled=True)
    z4 = z.reshape(4, 4, 128)
    m4 = mask.astype(F32).reshape(4, 4, 128)
    d4 = d.reshape(4, 2, 128)
    x4, f4, element = run_own(flags, z4, m4, f, h, weight, d4, x_own, parts)
    elements = lax.all_to_all(element, TIME, 0, 0, tiled=True)
    return run_smooth(flags, elements, d4, x4, f4)


def solution(mesh):
    fine = Mesh(mesh.devices.reshape(2, 4, 4, 2, 4), TIME + ("y",))
    t = P(TIME, None)
    ty = P(TIME, "y")
    return jax.shard_map(
        body,
        mesh=fine,
        in_specs=(t, t, P(), P(), P(), ty, P()),
        out_specs=(ty, ty),
        check_vma=False,
    )
```
